32 devices in a mesh: seq: 16 (over z, y, core), cp: 2 (over x).
Axes of the slice: x: 2, y: 2, z: 4, core: 2. Of those that a mesh axis runs over, the one named last changes fastest.
Arguments:
- inputs: bfloat16 [16384, 768], P(('seq', 'cp')), may hold values from -6 to 6
- doc_ids: int32 [16384], P(('seq', 'cp')), may hold values from 0 to 5, as said below
- cotangent: bfloat16 [16384, 768], P(('seq', 'cp')), may hold values from -6 to 6
- attn_norm_gain: bfloat16 [2, 768], P(None, ('seq', 'cp')), may hold values from 0.5 to 1.5
- attn_norm_bias: bfloat16 [2, 768], P(None, ('seq', 'cp')), may hold values from -1 to 1
- mlp_norm_gain: bfloat16 [2, 768], P(None, ('seq', 'cp')), may hold values from 0.5 to 1.5
- mlp_norm_bias: bfloat16 [2, 768], P(None, ('seq', 'cp')), may hold values from -1 to 1
- qkv_weight: bfloat16 [2, 768, 2304], P(None, ('seq', 'cp')), may hold values from -0.21875 to 0.21875
- qkv_bias: bfloat16 [2, 2304], P(None, ('seq', 'cp')), may hold values from -1 to 1
- dense_weight: bfloat16 [2, 768, 768], P(None, ('seq', 'cp')), may hold values from -1.25 to 1.25
- dense_bias: bfloat16 [2, 768], P(None, ('seq', 'cp')), may hold values from -1 to 1
- up_weight: bfloat16 [2, 768, 3072], P(None, ('seq', 'cp')), may hold values from -0.21875 to 0.21875
- up_bias: bfloat16 [2, 3072], P(None, ('seq', 'cp')), may hold values from -1 to 1
- down_weight: bfloat16 [2, 3072, 768], P(None, ('seq', 'cp')), may hold values from -0.109375 to 0.109375
- down_bias: bfloat16 [2, 768], P(None, ('seq', 'cp')), may hold values from -1 to 1
Outputs:
- layer_output: bfloat16 [16384, 768], P(('seq', 'cp'))
- input_grad: float32 [16384, 768], P(('seq', 'cp'))
- grad_attn_norm_gain: float32 [2, 768], P(None, ('seq', 'cp'))
- grad_attn_norm_bias: float32 [2, 768], P(None, ('seq', 'cp'))
- grad_mlp_norm_gain: float32 [2, 768], P(None, ('seq', 'cp'))
- grad_mlp_norm_bias: float32 [2, 768], P(None, ('seq', 'cp'))
- grad_qkv_weight: float32 [2, 768, 2304], P(None, ('seq', 'cp'))
- grad_qkv_bias: float32 [2, 2304], P(None, ('seq', 'cp'))
- grad_dense_weight: float32 [2, 768, 768], P(None, ('seq', 'cp'))
- grad_dense_bias: float32 [2, 768], P(None, ('seq', 'cp'))
- grad_up_weight: float32 [2, 768, 3072], P(None, ('seq', 'cp'))
- grad_up_bias: float32 [2, 3072], P(None, ('seq', 'cp'))
- grad_down_weight: float32 [2, 3072, 768], P(None, ('seq', 'cp'))
- grad_down_bias: float32 [2, 768], P(None, ('seq', 'cp'))
The draws below stay inside these ranges and needn't reach their ends.
Inputs may be any that keep to these rules, and one draw needn't show every extreme that they name: `doc_ids`: along each pack of 1024 tokens the numbers start at 0 and never fall; one document starts within the pack's first 512 tokens and ends within its last 512.
All inputs are finite; a program needn't handle non-finite values.
Results may differ from the reference program's by a relative error of at most 0.02.
Values may be sent and summed in bfloat16 or wider, within the bound.
No kernel may reach another device: no remote copies, remote signals or barrier semaphores. Data moves between devices by JAX's collectives and lax.ppermute only.
A program may use at most 320 MiB of HBM per device.

```python
import jax
import jax.numpy as jnp
from jax import lax

HEADS = 12
HEAD_DIM = 64
D = 768
FF = 3072
ROT_DIM = 16
LAYERS = 2
PACK = 1024
CP_ROWS = 512
GROUPS = 16
TOKENS = 16384


def draw_doc_ids(key, part):
    key = jax.random.fold_in(key, 7)

    def one_pack(pack_key):
        split_keys = jax.random.split(pack_key, 5)
        first_cut = jax.random.randint(split_keys[0], (), 1, CP_ROWS)
        last_cut = PACK - jax.random.randint(split_keys[1], (), 2, CP_ROWS)
        front_count = jax.random.randint(split_keys[2], (), 0, 4)
        front_cuts = jax.random.randint(split_keys[3], (3,), 0, first_cut)
        back_cuts = jax.random.randint(split_keys[4], (3,), last_cut, PACK - 1)
        chosen_cuts = jnp.where(jnp.arange(3, dtype=jnp.int32) < front_count, front_cuts, back_cuts)
        place_index = jnp.arange(PACK, dtype=jnp.int32)
        counted = (place_index >= first_cut).astype(jnp.int32) + (place_index >= last_cut).astype(jnp.int32)
        counted = counted + jnp.sum((place_index[:, None] > chosen_cuts[None, :]).astype(jnp.int32), axis=1)
        return counted
    return jax.vmap(one_pack)(jax.random.split(key, GROUPS)).reshape(TOKENS)


def with_spikes(drawn, rng, source, target, shards_of, factor):
    def block_of(dim):
        return (jnp.arange(drawn.shape[dim]) // (drawn.shape[dim] // shards_of)).reshape((-1,) + (1,) * (drawn.ndim - 1 - dim))

    one_side = jax.random.permutation(rng, shards_of)[block_of(target)]
    second = (block_of(target) + shards_of // 2) % shards_of
    return jnp.where((block_of(source) == one_side) | (block_of(source) == second), factor * drawn, drawn)


def level_of(stream_key, dims, cuts, low, top_value):
    factor_of, own = 1.0, jax.random.fold_in(stream_key, 6)
    for dim, blocks in cuts:
        draws = jnp.exp(jax.random.uniform(jax.random.fold_in(own, dim), (blocks,), jnp.float32, low / len(cuts), top_value / len(cuts)))
        factor_of = factor_of * jnp.repeat(draws, dims[dim] // blocks).reshape([-1 if axis == dim else 1 for axis in range(len(dims))])
    return factor_of


def bell_draw(stream_key, shape, deviation, reach, cuts=(), kind=jnp.bfloat16):
    drawn = jax.random.normal(stream_key, shape, jnp.float32) * deviation
    if len(cuts) > 0:
        drawn = level_of(stream_key, shape, cuts, -0.22, 0.18) * drawn
    return jnp.clip(drawn, min=-reach, max=reach).astype(kind)


def noise_with(own_key, extent, scale, limit, shards, heavy, kind=jnp.bfloat16):
    result = scale * jax.random.normal(own_key, extent, jnp.float32)
    if shards:
        result = result * level_of(own_key, extent, shards, -0.22, 0.18)
    return jnp.clip(with_spikes(result, jax.random.fold_in(own_key, 3), *heavy), -limit, limit).astype(kind)


def setup_inputs(seed: int = 0) -> dict:
    streams_of = jax.random.split(jax.random.key(seed), 16)
    return {
        "inputs": bell_draw(streams_of[0], (TOKENS, D), 1.0, 6.0, ((0, 32),)),
        "doc_ids": draw_doc_ids(jax.random.fold_in(streams_of[15], 71), 0),
        "cotangent": noise_with(streams_of[2], (TOKENS, D), 1.0, 6.0, ((0, 32),), (0, 1, 32, 2.75)),
        "attn_norm_gain": jnp.clip(1.0 + 0.1 * jax.random.normal(streams_of[3], (LAYERS, D), jnp.float32), 0.5, 1.5).astype(jnp.bfloat16),
        "attn_norm_bias": bell_draw(streams_of[4], (LAYERS, D), 0.2, 1.0, ((1, 32),)),
        "mlp_norm_gain": jnp.clip(1.0 + 0.1 * jax.random.normal(streams_of[5], (LAYERS, D), jnp.float32), 0.5, 1.5).astype(jnp.bfloat16),
        "mlp_norm_bias": bell_draw(streams_of[6], (LAYERS, D), 0.2, 1.0, ((1, 32),)),
        "qkv_weight": bell_draw(streams_of[7], (LAYERS, D, 3 * D), D ** -0.5, 0.21875, ((1, 32),)),
        "qkv_bias": bell_draw(streams_of[8], (LAYERS, 3 * D), 0.2, 1.0, ((1, 32),)),
        "dense_weight": bell_draw(streams_of[9], (LAYERS, D, D), (D // 32) ** -0.5, 1.25, ((1, 32),)),
        "dense_bias": bell_draw(streams_of[10], (LAYERS, D), 0.2, 1.0, ((1, 32),)),
        "up_weight": bell_draw(streams_of[11], (LAYERS, D, FF), D ** -0.5, 0.21875, ((1, 32),)),
        "up_bias": bell_draw(streams_of[12], (LAYERS, FF), 0.2, 1.0, ((1, 32),)),
        "down_weight": bell_draw(streams_of[13], (LAYERS, FF, D), FF ** -0.5, 0.109375, ((1, 32),)),
        "down_bias": bell_draw(streams_of[14], (LAYERS, D), 0.2, 1.0, ((1, 32),)),
    }


@jax.custom_vjp
def low(v):
    return lax.optimization_barrier(v.astype(jnp.bfloat16)).astype(jnp.float32)

@jax.custom_vjp
def low_back(v):
    return v

def low_keep(v):
    return (low(v), None)

def low_pass(kept, grad):
    return (grad,)

def back_keep(v):
    return (v, None)

def back_low(kept, grad):
    return (low(grad),)
low.defvjp(low_keep, low_pass)
low_back.defvjp(back_keep, back_low)
EPSILON = 1e-05
MASKED = -1e+30
HIGHEST = lax.Precision.HIGHEST

def product(left_side, right_side):
    return jnp.dot(left_side, right_side, precision=HIGHEST, preferred_element_type=jnp.float32)

def normalize(hidden):
    average = lax.optimization_barrier(jnp.mean(hidden, axis=-1, keepdims=True))
    centered = hidden - average
    variance = lax.optimization_barrier(jnp.mean(centered * centered, axis=-1, keepdims=True))
    return centered * lax.rsqrt(variance + EPSILON)

def rotary_tables(positions):
    half_rot = ROT_DIM // 2
    inverse = 10000.0 ** (-(jnp.arange(half_rot, dtype=jnp.float32) * 2.0 / ROT_DIM))
    angles = positions.astype(jnp.float32)[:, None] * jnp.concatenate([inverse, inverse])[None, :]
    return (jnp.cos(angles), jnp.sin(angles))

def rotate(vectors, cosine, sine_table):
    half_rot = ROT_DIM // 2
    turned = vectors[:, :, :ROT_DIM]
    swapped = jnp.concatenate([-turned[:, :, half_rot:], turned[:, :, :half_rot]], axis=2)
    rotated = turned * cosine[:, None, :] + swapped * sine_table[:, None, :]
    return jnp.concatenate([rotated, vectors[:, :, ROT_DIM:]], axis=2)

def attention(queries, key_rows, value_rows, doc_row):
    block_rows = min(512, PACK)
    columns = jnp.arange(PACK, dtype=jnp.int32)

    def one_block(offset):
        block_queries = lax.dynamic_slice_in_dim(queries, offset, block_rows, 0)
        row_index = offset + jnp.arange(block_rows, dtype=jnp.int32)
        row_docs = lax.dynamic_slice_in_dim(doc_row, offset, block_rows, 0)
        scores = jnp.einsum('qhd,khd->hqk', block_queries, key_rows, precision=HIGHEST, preferred_element_type=jnp.float32) * HEAD_DIM ** (-0.5)
        scores = low_back(scores)
        allowed = (columns[None, :] <= row_index[:, None]) & (doc_row[None, :] == row_docs[:, None])
        scores = jnp.where(allowed[None], scores, MASKED)
        probabilities = low(jax.nn.softmax(scores, axis=-1))
        return jnp.einsum('hqk,khd->qhd', probabilities, value_rows, precision=HIGHEST, preferred_element_type=jnp.float32)
    offsets = jnp.arange(PACK // block_rows, dtype=jnp.int32) * block_rows
    blocks = lax.map(jax.checkpoint(one_block), offsets)
    return blocks.reshape(PACK, HEADS * HEAD_DIM)

def pack_forward(hidden, doc_row, params):
    gain_attn, bias_attn, gain_mlp, bias_mlp, qkv_weight, qkv_bias, dense_weight, dense_bias, up_weight, up_bias, down_weight, down_bias = params
    place_index = jnp.arange(PACK, dtype=jnp.int32)
    starts = lax.optimization_barrier(jnp.sum((doc_row[None, :] < doc_row[:, None]).astype(jnp.int32), axis=1))
    cosine, sine_table = rotary_tables(place_index - starts)
    for layer_index in range(LAYERS):
        normed = normalize(hidden)
        attn_in = low(normed * gain_attn[layer_index] + bias_attn[layer_index])
        mlp_in = low(normed * gain_mlp[layer_index] + bias_mlp[layer_index])
        mixed_proj = low_back(product(attn_in, qkv_weight[layer_index]) + qkv_bias[layer_index])
        shaped = mixed_proj.reshape(PACK, 3, HEADS, HEAD_DIM)
        queries = low(rotate(shaped[:, 0], cosine, sine_table))
        key_rows = low(rotate(shaped[:, 1], cosine, sine_table))
        value_rows = low(shaped[:, 2])
        attended = low_back(low(attention(queries, key_rows, value_rows, doc_row)))
        branch_attn = low_back(product(attended, dense_weight[layer_index]) + dense_bias[layer_index])
        upper_pre = low_back(product(mlp_in, up_weight[layer_index]) + up_bias[layer_index])
        activated = low(jax.nn.gelu(upper_pre, approximate=False))
        branch_mlp = low_back(product(activated, down_weight[layer_index]) + down_bias[layer_index])
        hidden = hidden + branch_attn + branch_mlp
    return hidden

def reference(inputs, doc_ids, cotangent, attn_norm_gain, attn_norm_bias, mlp_norm_gain, mlp_norm_bias, qkv_weight, qkv_bias, dense_weight, dense_bias, up_weight, up_bias, down_weight, down_bias):
    params = tuple((weight.astype(jnp.float32) for weight in (attn_norm_gain, attn_norm_bias, mlp_norm_gain, mlp_norm_bias, qkv_weight, qkv_bias, dense_weight, dense_bias, up_weight, up_bias, down_weight, down_bias)))
    hidden = inputs.astype(jnp.float32).reshape(GROUPS, PACK, D)
    doc_rows = doc_ids.reshape(GROUPS, PACK)
    upstream = cotangent.astype(jnp.float32).reshape(GROUPS, PACK, D)

    def one_pack(totals, pack_item):
        pack_hidden, pack_docs, pack_grad = pack_item
        output, pullback = jax.vjp(lambda values, weights: pack_forward(values, pack_docs, weights), pack_hidden, params)
        grad_hidden, grad_params = pullback(pack_grad)
        totals = jax.tree.map(lambda summed_tree, added_tree: summed_tree + added_tree, totals, grad_params)
        return (totals, (output, grad_hidden))
    zero_grads = jax.tree.map(jnp.zeros_like, params)
    totals, (outputs, hidden_grads) = lax.scan(one_pack, zero_grads, (hidden, doc_rows, upstream))
    return (outputs.reshape(TOKENS, D).astype(jnp.bfloat16), hidden_grads.reshape(TOKENS, D), totals[0], totals[1], totals[2], totals[3], totals[4], totals[5], totals[6], totals[7], totals[8], totals[9], totals[10], totals[11])
```

```python
import functools

import jax
import jax.numpy as jnp
from jax import lax
from jax.experimental import pallas as pl
from jax.experimental.pallas import tpu as pltpu
from jax.sharding import PartitionSpec as P

HEADS = 12
HEAD_DIM = 64
ROT_DIM = 16
LAYERS = 2
LANES = 128
Q_BLOCK = 256

EPSILON = 1e-05
MASKED = -1e30
F32 = jnp.float32
BF16 = jnp.bfloat16
VMEM_LIMIT = 48 * 1024 * 1024


def pick(array, index, axis=0):
    return lax.dynamic_index_in_dim(array, index, axis, keepdims=False)


def dot_nn(left, right):
    return lax.dot_general(left, right, (((1,), (0,)), ((), ())), preferred_element_type=F32)


def dot_nt(left, right):
    return lax.dot_general(left, right, (((1,), (1,)), ((), ())), preferred_element_type=F32)


def dot_tn(left, right):
    return lax.dot_general(left, right, (((0,), (0,)), ((), ())), preferred_element_type=F32)


def cp_peer(array):
    return lax.ppermute(array, "cp", [(0, 1), (1, 0)])


def cp_gather(array):
    if lax.axis_size("cp") != 2:
        return lax.all_gather(array, "cp", axis=0, tiled=True)
    other = cp_peer(array)
    first = lax.axis_index("cp") == 0
    return jnp.concatenate([jnp.where(first, array, other), jnp.where(first, other, array)])


def cp_exchange(blocks):
    if lax.axis_size("cp") != 2:
        return lax.all_to_all(blocks, "cp", 0, 0)
    me = lax.axis_index("cp")
    mine = pick(blocks, me)
    other = cp_peer(pick(blocks, 1 - me).astype(BF16)).astype(blocks.dtype)
    first = me == 0
    return jnp.stack([jnp.where(first, mine, other), jnp.where(first, other, mine)])


def cp_sum(partial, low):
    if lax.axis_size("cp") != 2:
        return lax.psum(partial, "cp")
    return partial + cp_peer(low).astype(F32)


def cp_sends(partial, low, own_rows):
    if lax.axis_size("cp") != 2:
        if own_rows:
            return [(partial, lambda a: lax.psum_scatter(a, "cp", scatter_dimension=0, tiled=True))]
        return [(partial, lambda a: lax.psum(a, "cp"))]
    if own_rows:
        rows = partial.shape[0] // 2
        other = (1 - lax.axis_index("cp")) * rows
        low = lax.dynamic_slice_in_dim(low, other, rows, 0)
    return [(low, cp_peer)]


def cp_total(partial, brought, own_rows):
    if lax.axis_size("cp") != 2:
        return brought[0]
    if own_rows:
        rows = partial.shape[0] // 2
        partial = lax.dynamic_slice_in_dim(partial, lax.axis_index("cp") * rows, rows, 0)
    return partial + brought[0].astype(F32)


def cp_sum_rows(partial, low):
    if lax.axis_size("cp") != 2:
        return lax.psum_scatter(partial, "cp", scatter_dimension=0, tiled=True)
    rows = partial.shape[0] // 2
    me = lax.axis_index("cp")
    other = cp_peer(lax.dynamic_slice_in_dim(low, (1 - me) * rows, rows, 0))
    return lax.dynamic_slice_in_dim(partial, me * rows, rows, 0) + other.astype(F32)


def seq_shift(array, target):
    count = lax.axis_size("seq")
    return lax.ppermute(array, "seq", [(i, target(i) % count) for i in range(count)])


def ring_next(array):
    return seq_shift(array, lambda i: i + 4)


def pair_swap(array):
    return seq_shift(array, lambda i: i ^ 2)


def core_swap(array):
    return seq_shift(array, lambda i: i ^ 1)


def sum_everywhere(array):
    count = lax.axis_size("seq")
    if lax.axis_size("cp") != 2 or count & (count - 1):
        return lax.psum(array, ("seq", "cp"))
    array = array + cp_peer(array)
    bit = 1
    while bit < count:
        array = array + seq_shift(array, lambda i, bit=bit: i ^ bit)
        bit *= 2
    return array


def seq_place():
    me = lax.axis_index("seq")
    return me // 4, (me // 2) % 2, me % 2


def seq_gather(block, later):
    count = lax.axis_size("seq")
    if count % 8:
        return lax.all_gather(block, "seq", axis=0, tiled=True), later
    rings = count // 4
    ring, pair, core = seq_place()
    result = jnp.zeros((rings, 2, 2) + block.shape, block.dtype)
    held, waiting = block, []
    for step in range(rings):
        following = ring_next(held) if step < rings - 1 else None
        other = pair_swap(held)
        waiting.append(
            jnp.where(pair == 0, jnp.stack([held, other]), jnp.stack([other, held]))
        )
        held = following
        if step == rings - 2:
            held, later = lax.optimization_barrier((held, later))
        if step % 2 == 0:
            continue
        both = jnp.stack(waiting)
        sibling = core_swap(both)
        quads = jnp.where(
            core == 0, jnp.stack([both, sibling], axis=2), jnp.stack([sibling, both], axis=2)
        )
        for index in range(2):
            result = lax.dynamic_update_slice(
                result,
                quads[index : index + 1],
                ((ring - step + 1 - index) % rings,) + (0,) * (quads.ndim - 1),
            )
        waiting = []
    return result.reshape((count * block.shape[0],) + block.shape[1:]), later


def turn(block, cosine, sine_up, sine_down):
    return (
        block * cosine
        + pltpu.roll(block, LANES - ROT_DIM // 2, 1) * sine_up
        + pltpu.roll(block, ROT_DIM // 2, 1) * sine_down
    )


def turn_back(block, cosine, sine_up, sine_down):
    return (
        block * cosine
        + pltpu.roll(block * sine_up, ROT_DIM // 2, 1)
        + pltpu.roll(block * sine_down, LANES - ROT_DIM // 2, 1)
    )


def head_lanes(shape, head):
    lane = lax.broadcasted_iota(jnp.int32, shape, 1)
    return (lane < HEAD_DIM) if head == 0 else (lane >= HEAD_DIM)


def keys_first(rows):
    key_place = lax.broadcasted_iota(jnp.int32, (rows, rows), 0)
    query_place = lax.broadcasted_iota(jnp.int32, (rows, rows), 1)
    return key_place <= query_place


def forward_kernel(
    q_ref, k_ref, v_ref, query_pen, key_pen, out_ref, stat_ref, turned_t,
):
    rows = q_ref.shape[0]
    queries, keys, values = q_ref[...], k_ref[...], v_ref[...]
    value_t = values.astype(F32).T.astype(BF16)
    block = min(Q_BLOCK, rows)
    causal = keys_first(block)
    for head in range(2):
        lanes = head_lanes((rows, LANES), head)
        head_q = jnp.where(lanes, queries, query_pen[...])
        head_k = jnp.where(lanes, keys, key_pen[...])
        head_v = value_t[head * HEAD_DIM : (head + 1) * HEAD_DIM, :]
        for start in range(0, rows, block):
            stop = start + block
            scores = dot_nt(head_k[:stop], head_q[start:stop])
            last = jnp.where(causal, scores[start:], MASKED)
            scores = last if start == 0 else jnp.concatenate([scores[:start], last])
            top = jnp.max(scores, axis=0, keepdims=True)
            terms = jnp.exp(scores - top)
            total = jnp.sum(terms, axis=0, keepdims=True)
            summed = dot_nn(head_v[:, :stop], terms.astype(BF16))
            turned_t[head * HEAD_DIM : (head + 1) * HEAD_DIM, start:stop] = summed / total
            stat_ref[0, head : head + 1, start:stop] = top + jnp.log(total)
    out_ref[...] = turned_t[...].T.astype(BF16)


def attention_forward(queries, keys, values, penalties):
    rows, width = queries.shape
    pairs = width // LANES
    whole = pl.BlockSpec((rows, LANES), lambda p: (0, 0))
    column = pl.BlockSpec((rows, LANES), lambda p: (0, p))
    return pl.pallas_call(
        forward_kernel,
        grid=(pairs,),
        in_specs=[column] * 3 + [whole] * 2,
        out_specs=[column, pl.BlockSpec((1, 2, rows), lambda p: (p, 0, 0))],
        out_shape=[
            jax.ShapeDtypeStruct((rows, width), BF16),
            jax.ShapeDtypeStruct((pairs, 2, rows), F32),
        ],
        scratch_shapes=[pltpu.VMEM((LANES, rows), F32)],
        compiler_params=pltpu.CompilerParams(vmem_limit_bytes=VMEM_LIMIT),
        cost_estimate=pl.CostEstimate(
            flops=pairs * rows * rows * LANES,
            bytes_accessed=rows * width,
            transcendentals=0,
        ),
        name="attention_forward",
    )(queries, keys, values, *penalties)


def backward_kernel(
    q_ref, k_ref, v_ref, out_ref, grad_ref, stat_ref, cos_ref, up_ref, down_ref, query_pen, key_pen,
    mixed_ref, delta_t, grad_q,
):
    rows = q_ref.shape[0]
    width = mixed_ref.shape[1] // 3
    pair = pl.program_id(0)
    queries, keys, values, grads = q_ref[...], k_ref[...], v_ref[...], grad_ref[...]
    products = (grads.astype(F32) * out_ref[...].astype(F32)).T
    for head in range(2):
        delta_t[head : head + 1, :] = jnp.sum(
            products[head * HEAD_DIM : (head + 1) * HEAD_DIM, :], axis=0, keepdims=True
        )
    tables = (cos_ref[...], up_ref[...], down_ref[...])
    grad_q[...] = jnp.zeros_like(grad_q)
    block = min(Q_BLOCK, rows)
    causal = keys_first(block)
    none = jnp.zeros((rows, LANES), BF16)
    heads = []
    for head in range(2):
        lanes = head_lanes((rows, LANES), head)
        heads.append(
            (
                jnp.where(lanes, queries, query_pen[...]),
                jnp.where(lanes, keys, key_pen[...]),
                jnp.where(lanes, queries, none),
                jnp.where(lanes, keys, none),
                jnp.where(lanes, values, none),
                jnp.where(lanes, grads, none),
            )
        )
    for start in range(0, rows, block):
        stop = start + block
        grad_k, grad_v = None, None
        for head, (score_q, score_k, head_q, head_k, head_v, head_g) in enumerate(heads):
            scores = dot_nt(score_k[start:stop], score_q[start:])
            first = jnp.where(causal, scores[:, :block], MASKED)
            scores = (
                first if stop == rows else jnp.concatenate([first, scores[:, block:]], axis=1)
            )
            weights = jnp.exp(scores - stat_ref[0, head : head + 1, start:])
            grad_p = dot_nt(head_v[start:stop], head_g[start:])
            grad_s = (weights * (grad_p - delta_t[head : head + 1, start:])).astype(BF16)
            more_v = dot_nn(weights.astype(BF16), head_g[start:])
            more_k = dot_nn(grad_s, head_q[start:])
            grad_v = more_v if grad_v is None else grad_v + more_v
            grad_k = more_k if grad_k is None else grad_k + more_k
            grad_q[start:, :] += dot_tn(grad_s, head_k[start:stop])
        block_tables = tuple(table[start:stop] for table in tables)
        mixed_ref[start:stop, pl.ds(pl.multiple_of(width + pair * LANES, LANES), LANES)] = (
            turn_back(grad_k, *block_tables).astype(BF16)
        )
        mixed_ref[start:stop, pl.ds(pl.multiple_of(2 * width + pair * LANES, LANES), LANES)] = (
            grad_v.astype(BF16)
        )
    mixed_ref[:, pl.ds(pl.multiple_of(pair * LANES, LANES), LANES)] = turn_back(
        grad_q[...] * HEAD_DIM**-0.5, *tables
    ).astype(BF16)


def attention_backward(queries, keys, values, attended, grad_attended, stats, tables, penalties):
    rows, width = queries.shape
    pairs = width // LANES
    whole = pl.BlockSpec((rows, LANES), lambda p: (0, 0))
    column = pl.BlockSpec((rows, LANES), lambda p: (0, p))
    stat = pl.BlockSpec((1, 2, rows), lambda p: (p, 0, 0))
    return pl.pallas_call(
        backward_kernel,
        grid=(pairs,),
        in_specs=[column] * 5 + [stat] + [whole] * 5,
        out_specs=pl.BlockSpec((rows, 3 * width), lambda p: (0, 0)),
        out_shape=jax.ShapeDtypeStruct((rows, 3 * width), BF16),
        scratch_shapes=[pltpu.VMEM((2, rows), F32), pltpu.VMEM((rows, LANES), F32)],
        compiler_params=pltpu.CompilerParams(vmem_limit_bytes=VMEM_LIMIT),
        cost_estimate=pl.CostEstimate(
            flops=pairs * rows * rows * LANES,
            bytes_accessed=rows * width,
            transcendentals=0,
        ),
        name="attention_backward",
    )(queries, keys, values, attended, grad_attended, stats, *tables, *penalties)


ROW_BLOCK = 256


def layer_norm(hidden):
    average = jnp.mean(hidden, axis=-1, keepdims=True)
    centered = hidden - average
    variance = jnp.mean(centered * centered, axis=-1, keepdims=True)
    inverse_std = lax.rsqrt(variance + EPSILON)
    return centered * inverse_std, inverse_std


def load_parts(parts, semaphores):
    copies = [
        pltpu.make_async_copy(source, target, semaphores.at[index])
        for index, (source, target) in enumerate(parts)
    ]
    first = pl.program_id(0) == 0

    @pl.when(first)
    def _():
        for copy in copies:
            copy.start()

    def wait(*indices):
        @pl.when(first)
        def _():
            for index in indices:
                copies[index].wait()

    return wait


def down_parts(source, sizes, target):
    if sizes.slabs == 0:
        return [(source, target)]
    first, rows, features = sizes.split + sizes.hidden, sizes.rows, sizes.features
    parts = []
    for group in range(sizes.groups):
        for slab in range(sizes.slabs):
            lanes = slice(first + slab * features, first + (slab + 1) * features)
            start = (group * sizes.slabs + slab) * rows
            parts.append(
                (
                    source.at[group * rows : (group + 1) * rows, lanes],
                    target.at[start : start + rows, :],
                )
            )
    return parts


def project_kernel(
    sizes, hidden, gain, bias, qkv_bias, whole, cos_ref, up_ref, down_ref,
    attn_in, q_ref, k_ref, v_ref, qkv, semaphores,
):
    width = sizes.width
    wait = load_parts([(whole.at[:, : 3 * width], qkv)], semaphores)
    normed, _ = layer_norm(hidden[...])
    low = (normed * gain[...] + bias[...]).astype(BF16)
    attn_in[...] = low
    wait(0)
    tables = (cos_ref[...], up_ref[...], down_ref[...])
    mixed = dot_nn(low, qkv[...]) + qkv_bias[...]
    for start in range(0, width, LANES):
        lanes = slice(start, start + LANES)
        turned = turn(mixed[:, start : start + LANES], *tables).astype(BF16)
        q_ref[:, lanes] = turned * jnp.asarray(HEAD_DIM**-0.5, BF16)
        first = width + start
        k_ref[:, lanes] = turn(mixed[:, first : first + LANES], *tables).astype(BF16)
    v_ref[...] = mixed[:, 2 * width :].astype(BF16)


def row_call(kernel, sizes, rows, operands, results, scratch, copies, flops, name):
    block = min(ROW_BLOCK, rows)

    def spec(shape, kind):
        if kind == "hbm":
            return pl.BlockSpec(memory_space=pl.ANY)
        if kind == "rows":
            return pl.BlockSpec((block, shape[1]), lambda i: (i, 0))
        return pl.BlockSpec(shape, lambda i: (0, 0))

    return pl.pallas_call(
        functools.partial(kernel, sizes),
        grid=(rows // block,),
        in_specs=[spec(array.shape, kind) for array, kind in operands],
        out_specs=[spec(shape, kind) for shape, _, kind in results],
        out_shape=[jax.ShapeDtypeStruct(shape, dtype) for shape, dtype, _ in results],
        scratch_shapes=scratch + [pltpu.SemaphoreType.DMA((copies,))],
        compiler_params=pltpu.CompilerParams(vmem_limit_bytes=VMEM_LIMIT),
        cost_estimate=pl.CostEstimate(
            flops=flops // 8, bytes_accessed=rows * sizes.features, transcendentals=0
        ),
        name=name,
    )(*[array for array, _ in operands])


def project(hidden, weights, tables, sizes):
    rows, features, width = hidden.shape[0], sizes.features, sizes.width
    return row_call(
        project_kernel, sizes, rows,
        [(hidden, "rows"), (weights["gain_attn"], "all"), (weights["bias_attn"], "all"),
         (weights["qkv_bias"], "all"), (weights["whole"], "hbm")]
        + [(table, "rows") for table in tables],
        [((rows, features), BF16, "rows")] + [((rows, width), BF16, "rows")] * 3,
        [pltpu.VMEM((features, 3 * width), BF16)], 1,
        2 * rows * features * 3 * width, "project",
    )


ERFC_TERMS = (
    0.17087277, -0.82215223, 1.48851587, -1.13520398, 0.27886807,
    -0.18628806, 0.09678418, 0.37409196, 1.00002368, -1.26551223,
)


def gelu_and_slope(upper):
    size = jnp.abs(upper) * 0.5**0.5
    inverse = 1.0 / (1.0 + 0.5 * size)
    series = inverse * ERFC_TERMS[0] + ERFC_TERMS[1]
    for term in ERFC_TERMS[2:]:
        series = series * inverse + term
    square = size * size
    tail = 0.5 * inverse * jnp.exp(series - square)
    below = jnp.where(upper < 0, tail, 1.0 - tail)
    slope = below + upper * (jnp.exp(-square) * 0.3989422804014327)
    return upper * below, slope


def branches_kernel(
    sizes, hidden, attended, gain, bias, up_bias, whole, down_source, dense,
    mlp_in, activated, slope_ref, partial, partial_low, up, down, upper, semaphores,
):
    up_part = (whole.at[:, sizes.split : sizes.split + sizes.hidden], up)
    downs = down_parts(down_source, sizes, down)
    wait = load_parts([up_part] + downs, semaphores)
    normed, _ = layer_norm(hidden[...])
    low = (normed * gain[...] + bias[...]).astype(BF16)
    mlp_in[...] = low
    total = dot_nn(attended[...], dense[...])
    wait(0)
    upper[...] = dot_nn(low, up[...]) + up_bias[...]
    units = upper.shape[1]
    tile = 512 if units % 512 == 0 else LANES

    @pl.loop(0, upper.shape[0], step=16)
    def _(first):
        rows = pl.ds(pl.multiple_of(first, 16), 16)
        for start in range(0, units, tile):
            lanes = slice(start, start + tile)
            act, slope = gelu_and_slope(upper[rows, lanes])
            activated[rows, lanes] = act.astype(BF16)
            slope_ref[rows, lanes] = slope.astype(BF16)

    wait(*range(1, 1 + len(downs)))
    total = total + dot_nn(activated[...], down[...])
    partial[...] = total
    partial_low[...] = total.astype(BF16)


def branches(hidden, attended, weights, sizes):
    rows, features, units, width = hidden.shape[0], sizes.features, sizes.hidden, sizes.width
    return row_call(
        branches_kernel, sizes, rows,
        [(hidden, "rows"), (attended, "rows"), (weights["gain_mlp"], "all"),
         (weights["bias_mlp"], "all"), (weights["up_bias"], "all"), (weights["whole"], "hbm"),
         (weights["down"], "hbm"), (weights["dense"], "all")],
        [((rows, features), BF16, "rows")] + [((rows, units), BF16, "rows")] * 2
        + [((rows, features), F32, "rows"), ((rows, features), BF16, "rows")],
        [pltpu.VMEM((features, units), BF16), pltpu.VMEM((units, features), BF16),
         pltpu.VMEM((min(ROW_BLOCK, rows), units), F32)],
        1 + sizes.down_copies, 2 * rows * features * (2 * units + width), "branches",
    )


def add_sums(ref, index, block):
    ref[index : index + 1, :] += jnp.sum(block, axis=0, keepdims=True)


def branches_back_kernel(
    sizes, low_ref, slope, hidden, gain, whole, down_source, dense,
    grad_attended, grad_upper, grad_mlp, sums, unit_sums, up, down, semaphores,
):
    downs = down_parts(down_source, sizes, down)
    up_part = (whole.at[:, sizes.split : sizes.split + sizes.hidden], up)
    wait = load_parts(downs + [up_part], semaphores)

    @pl.when(pl.program_id(0) == 0)
    def _():
        sums[...] = jnp.zeros_like(sums)
        unit_sums[...] = jnp.zeros_like(unit_sums)

    low = low_ref[...]
    grad_attended[...] = dot_nt(low, dense[...]).astype(BF16)
    normed, _ = layer_norm(hidden[...])
    wait(*range(len(downs)))
    upper = (dot_nt(low, down[...]) * slope[...].astype(F32)).astype(BF16)
    grad_upper[...] = upper
    add_sums(unit_sums, 0, upper.astype(F32))
    wait(len(downs))
    grad = dot_nt(upper, up[...])
    add_sums(sums, 0, grad * normed)
    add_sums(sums, 1, grad)
    add_sums(sums, 2, low.astype(F32))
    grad_mlp[...] = grad * gain[...]


def branches_back(low, slope, hidden, weights, sizes):
    rows, features, units, width = hidden.shape[0], sizes.features, sizes.hidden, sizes.width
    return row_call(
        branches_back_kernel, sizes, rows,
        [(low, "rows"), (slope, "rows"), (hidden, "rows"), (weights["gain_mlp"], "all"),
         (weights["whole"], "hbm"), (weights["down"], "hbm"), (weights["dense"], "all")],
        [((rows, width), BF16, "rows"), ((rows, units), BF16, "rows"),
         ((rows, features), F32, "rows"), ((8, features), F32, "all"), ((8, units), F32, "all")],
        [pltpu.VMEM((features, units), BF16), pltpu.VMEM((units, features), BF16)],
        1 + sizes.down_copies, 2 * rows * features * (2 * units + width), "branches_back",
    )


def project_back_kernel(
    sizes, mixed, grad_mlp, hidden, gain, whole, partial, partial_low, sums, mixed_sums, qkv,
    semaphores,
):
    wait = load_parts([(whole.at[:, : 3 * sizes.width], qkv)], semaphores)

    @pl.when(pl.program_id(0) == 0)
    def _():
        sums[...] = jnp.zeros_like(sums)
        mixed_sums[...] = jnp.zeros_like(mixed_sums)

    normed, inverse_std = layer_norm(hidden[...])
    add_sums(mixed_sums, 0, mixed[...].astype(F32))
    wait(0)
    grad = dot_nt(mixed[...], qkv[...])
    add_sums(sums, 0, grad * normed)
    add_sums(sums, 1, grad)
    grad = grad * gain[...] + grad_mlp[...]
    centered = (
        grad
        - jnp.mean(grad, axis=-1, keepdims=True)
        - normed * jnp.mean(grad * normed, axis=-1, keepdims=True)
    )
    grad = inverse_std * centered
    partial[...] = grad
    partial_low[...] = grad.astype(BF16)


def project_back(grad_mixed, grad_mlp, hidden, weights, sizes):
    rows, features, width = hidden.shape[0], sizes.features, sizes.width
    return row_call(
        project_back_kernel, sizes, rows,
        [(grad_mixed, "rows"), (grad_mlp, "rows"), (hidden, "rows"),
         (weights["gain_attn"], "all"), (weights["whole"], "hbm")],
        [((rows, features), F32, "rows"), ((rows, features), BF16, "rows"),
         ((8, features), F32, "all"), ((8, 3 * width), F32, "all")],
        [pltpu.VMEM((features, 3 * width), BF16)], 1,
        2 * rows * features * 3 * width, "project_back",
    )


def lay_out(refs, widths, sizes, store):
    first = 0
    for ref, width in zip(refs, widths):
        if width is None:
            for slab in range(sizes.slabs):
                rows = slice(slab * sizes.rows, (slab + 1) * sizes.rows)
                store(ref[rows, :], slice(first, first + sizes.features))
                first += sizes.features
        else:
            store(ref[...], slice(first, first + width))
            first += width


def pack_kernel(sizes, widths, place, *refs):
    packed = refs[-1]

    def store(block, lanes):
        packed[0, 0, :, lanes] = block

    lay_out(refs[:-1], widths, sizes, store)


def first_sum_kernel(sizes, widths, place, *refs):
    count = len(widths)
    sibling_sent, sibling_mine, sent, mine = refs[2 * count :]

    def store_sent(block, lanes):
        total = block.astype(F32) + sibling_sent[0, 0, :, lanes].astype(F32)
        sent[0, :, lanes] = total.astype(BF16)

    def store_mine(block, lanes):
        mine[0, :, lanes] = block.astype(F32) + sibling_mine[0, 0, :, lanes].astype(F32)

    lay_out(refs[:count], widths, sizes, store_sent)
    lay_out(refs[count : 2 * count], widths, sizes, store_mine)


class Scatter:
    def __init__(self, parts, sizes):
        self.sizes, self.stage, self.operands, self.result = sizes, 0, [], None
        self.rings = sizes.groups // 4
        self.kernels = sizes.groups % 8 == 0 and sizes.rows % 16 == 0
        self.parts = [
            part if owned else (part if part.shape[0] == sizes.features else sizes.pack_down(part))
            for part, owned in ((part, self.kernels) for part in parts)
        ]
        self.widths = [
            part.shape[1] if part.shape[0] == sizes.features else None for part in self.parts
        ]
        self.columns = sum(part.size for part in self.parts) // sizes.features
        if not self.kernels:
            packed = jnp.concatenate(self.parts, axis=1)
            summed = lax.psum_scatter(packed, "seq", scatter_dimension=0, tiled=True)
            self.result = summed.astype(F32)
            return
        ring, pair, core = seq_place()
        self.place = jnp.stack([ring, pair, core]).astype(jnp.int32)
        self.operands = [self.pack()]

    def cost(self):
        return pl.CostEstimate(
            flops=0, bytes_accessed=self.sizes.features * self.columns * 4, transcendentals=0
        )

    def specs(self, index):
        rows = self.sizes.rows
        return [
            pl.BlockSpec((rows * (self.sizes.slabs if width is None else 1), part.shape[1]), index)
            for part, width in zip(self.parts, self.widths)
        ]

    def pack(self):
        def other(ring, pair, place):
            return ((ring * 2 + pair) * 2 + 1 - place[2], 0)

        rows, rings = self.sizes.rows, self.rings
        return pl.pallas_call(
            functools.partial(pack_kernel, self.sizes, self.widths),
            grid_spec=pltpu.PrefetchScalarGridSpec(
                num_scalar_prefetch=1,
                grid=(rings, 2),
                in_specs=self.specs(other),
                out_specs=pl.BlockSpec((1, 1, rows, self.columns), lambda r, p, place: (r, p, 0, 0)),
            ),
            out_shape=jax.ShapeDtypeStruct((rings, 2, rows, self.columns), BF16),
            compiler_params=pltpu.CompilerParams(vmem_limit_bytes=VMEM_LIMIT),
            cost_estimate=self.cost(),
            name="pack_terms",
        )(self.place, *self.parts)

    def first_sum(self):
        rows, rings, columns = self.sizes.rows, self.rings, self.columns

        def ring_of(step, place):
            return lax.rem(place[0] + 2 * rings - 1 - step, rings)

        def own(pair_of):
            return lambda step, place: (
                (ring_of(step, place) * 2 + pair_of(place)) * 2 + place[2],
                0,
            )

        def sibling(pair_of):
            return pl.BlockSpec(
                (1, 1, rows, columns),
                lambda step, place: (ring_of(step, place), pair_of(place), 0, 0),
            )

        def away(place):
            return 1 - place[1]

        def home(place):
            return place[1]

        step_block = pl.BlockSpec((1, rows, columns), lambda step, place: (step, 0, 0))
        return pl.pallas_call(
            functools.partial(first_sum_kernel, self.sizes, self.widths),
            grid_spec=pltpu.PrefetchScalarGridSpec(
                num_scalar_prefetch=1,
                grid=(rings,),
                in_specs=self.specs(own(away))
                + self.specs(own(home))
                + [sibling(away), sibling(home)],
                out_specs=[step_block, step_block],
            ),
            out_shape=[
                jax.ShapeDtypeStruct((rings, rows, columns), BF16),
                jax.ShapeDtypeStruct((rings, rows, columns), F32),
            ],
            compiler_params=pltpu.CompilerParams(vmem_limit_bytes=VMEM_LIMIT),
            cost_estimate=self.cost(),
            name="first_sum",
        )(self.place, *self.parts, *self.parts, self.sibling, self.sibling)

    def launch(self, operands):
        if self.stage == 0:
            return [core_swap(operands[0])]
        if self.stage == 1:
            self.arrived = [pair_swap(operand) for operand in operands]
            return self.arrived[:1]
        return [ring_next(operands[0])]

    def land(self, received):
        if self.stage == 0:
            self.sibling = received[0]
        elif self.stage == 1:
            self.arrived[0] = received[0]
        else:
            self.received = received[0]
        self.stage += 1

    def prepare(self):
        if self.result is not None or self.stage == 0:
            return
        half = self.rings // 2
        if self.stage == 1:
            sent, self.mine = self.first_sum()
            self.operands = [sent[:half], sent[half:]]
            return
        step = self.stage - 2
        total = self.mine[step] + self.arrived[step // half][step % half].astype(F32)
        if step > 0:
            total = total + self.received.astype(F32)
        if step == self.rings - 1:
            self.result, self.operands = total, []
        else:
            self.operands = [total.astype(BF16)]


def beside(scatters, inputs, compute, sends=()):
    scatters = [scatter for scatter in scatters if scatter.result is None]
    for scatter in scatters:
        scatter.prepare()
    scatters = [scatter for scatter in scatters if scatter.result is None]
    operands = [scatter.operands for scatter in scatters]
    inputs, operands, sent = lax.optimization_barrier(
        (tuple(inputs), operands, [operand for operand, _ in sends])
    )
    landing = [scatter.launch(operand) for scatter, operand in zip(scatters, operands)]
    brought = [transfer(operand) for operand, (_, transfer) in zip(sent, sends)]
    short = [scatter.stage == 0 for scatter in scatters]
    tied = [received for received, is_short in zip(landing, short) if is_short]
    results, tied, brought = lax.optimization_barrier((compute(*inputs), tied, brought))
    for scatter, received, is_short in zip(scatters, landing, short):
        scatter.land(tied.pop(0) if is_short else received)
    return results, brought


def finish(scatters):
    while any(scatter.result is None for scatter in scatters):
        for scatter in scatters:
            if scatter.result is None:
                scatter.prepare()
            if scatter.result is None:
                scatter.land(scatter.launch(scatter.operands))


def rotary_tables(positions):
    half_rot = ROT_DIM // 2
    inverse = 10000.0 ** (-(jnp.arange(half_rot, dtype=F32) * 2.0 / ROT_DIM))
    angles = positions.astype(F32)[:, None] * inverse[None, :]
    cosine, sine = jnp.cos(angles), jnp.sin(angles)
    rows = positions.shape[0]
    rest = HEAD_DIM - ROT_DIM
    zeros = jnp.zeros_like(sine)
    still = jnp.zeros((rows, rest), F32)
    cosine = jnp.concatenate([cosine, cosine, jnp.ones((rows, rest), F32)] * 2, axis=1)
    sine_up = jnp.concatenate([-sine, zeros, still] * 2, axis=1)
    sine_down = jnp.concatenate([zeros, sine, still] * 2, axis=1)
    return cosine, sine_up, sine_down


def document_penalties(docs):
    slots = jnp.arange(LANES, dtype=jnp.int32) % HEAD_DIM
    same = docs[:, None] == slots[None, :]
    return jnp.where(same, 0.0, MASKED).astype(BF16), same.astype(BF16)


def pad_heads(array, axis, sizes):
    missing = sizes.members * sizes.width - HEADS * HEAD_DIM
    if missing == 0:
        return array
    pads = [(0, 0)] * array.ndim
    pads[axis] = (0, missing)
    return jnp.pad(array, pads)


class Sizes:
    def __init__(self, features, hidden):
        self.members, self.groups = lax.axis_size("cp"), lax.axis_size("seq")
        per_member = -(-HEADS // self.members)
        self.padded = self.members * (per_member + per_member % 2)
        self.width = self.padded // self.members * HEAD_DIM
        self.features = features
        self.rows = features // self.groups
        owned = hidden // (self.members * self.groups)
        self.slabs = owned // self.rows if owned % self.rows == 0 and self.rows % 16 == 0 else 0
        self.down_copies = max(self.slabs * self.groups, 1)
        self.hidden = hidden // self.members
        self.ratio = hidden // features
        self.split = 3 * self.width + features
        self.owned = features // (self.members * self.groups)

    def pack_down(self, rows):
        if self.slabs == 0:
            return rows.reshape(-1, self.hidden)
        rows = rows.reshape(-1, self.slabs, self.rows, self.features)
        return jnp.transpose(rows, (0, 2, 1, 3)).reshape(-1, self.hidden)

    def unpack_down(self, packed):
        if self.slabs == 0:
            return packed.reshape(-1, self.features)
        packed = packed.reshape(-1, self.rows, self.slabs, self.features)
        return jnp.transpose(packed, (0, 2, 1, 3)).reshape(-1, self.features)


def to_users(rows, sizes, back=False):
    count = sizes.members * sizes.groups
    moves = [(i, (i % sizes.groups) * sizes.members + i // sizes.groups) for i in range(count)]
    if back:
        moves = [(target, source) for source, target in moves]
    return lax.ppermute(rows, ("seq", "cp"), moves)


def cut_columns(params, sizes):
    qkv_weight, dense_weight, up_weight = params[4], params[6], params[8]
    layers, rows, members = qkv_weight.shape[0], qkv_weight.shape[1], sizes.members
    qkv = pad_heads(qkv_weight.reshape(layers, rows, 3, HEADS * HEAD_DIM), 3, sizes)
    shares = []
    for member in range(members):
        heads = slice(member * sizes.width, (member + 1) * sizes.width)
        units = slice(member * sizes.hidden, (member + 1) * sizes.hidden)
        shares.append(
            jnp.concatenate(
                [qkv[:, :, part, heads] for part in range(3)]
                + [dense_weight, up_weight[:, :, units]],
                axis=2,
            )
        )
    return jnp.stack(shares)


def fetch_layers(params, exchanged, down, sizes, tokens):
    packed = [
        jnp.concatenate(
            [
                exchanged[:, layer].reshape(-1, exchanged.shape[-1]),
                sizes.pack_down(down[layer]),
            ],
            axis=1,
        )
        for layer in range(LAYERS)
    ]
    first, later = seq_gather(packed[0], packed[1:] + [tokens])
    fetched = [unpack_layer(first, sizes)]
    for block in later[:-1]:
        whole = lax.all_gather(block, "seq", axis=0, tiled=True)
        fetched.append(unpack_layer(whole, sizes))
    return fetched, later[-1]


def fetch_vectors(params, sizes):
    vectors = [params[i] for i in (0, 1, 2, 3, 7, 11, 5, 9)]
    me = lax.axis_index("cp")
    owner = lax.axis_index("seq") * sizes.members + me
    layers = vectors[0].shape[0]
    placed = [
        lax.dynamic_update_slice(
            jnp.zeros((layers, vector.shape[1] * sizes.members * sizes.groups), BF16),
            vector,
            (0, owner * vector.shape[1]),
        )
        for vector in vectors
    ]
    widths = [vector.shape[1] for vector in placed]
    every = sum_everywhere(jnp.concatenate(placed, axis=1)).astype(F32)
    results = []
    for layer in range(layers):
        first, arrays = 0, []
        for width in widths:
            arrays.append(every[layer : layer + 1, first : first + width])
            first += width
        gain_attn, bias_attn, gain_mlp, bias_mlp, dense_bias, down_bias, qkv_bias, up_bias = arrays
        qkv_bias = pad_heads(qkv_bias.reshape(3, HEADS * HEAD_DIM), 1, sizes)
        qkv_bias = lax.dynamic_slice_in_dim(qkv_bias, me * sizes.width, sizes.width, 1)
        up_bias = lax.dynamic_slice_in_dim(up_bias, me * sizes.hidden, sizes.hidden, 1)
        results.append(
            {
                "qkv_bias": qkv_bias.reshape(1, -1), "up_bias": up_bias,
                "gain_attn": gain_attn, "bias_attn": bias_attn,
                "gain_mlp": gain_mlp, "bias_mlp": bias_mlp,
                "out_bias": dense_bias + down_bias,
            }
        )
    return results


def unpack_layer(whole, sizes):
    split, features = sizes.split, sizes.features
    dense = whole[:, 3 * sizes.width : split]
    down = whole if sizes.slabs else sizes.unpack_down(whole[:, split + sizes.hidden :])
    dense = jnp.pad(dense, ((0, sizes.members * sizes.width - features), (0, 0)))
    dense = lax.dynamic_slice_in_dim(
        dense, lax.axis_index("cp") * sizes.width, sizes.width, 0
    )
    return {"whole": whole, "dense": dense, "down": down}


def layer_forward(hidden, weights, tables, penalties, sizes):
    attn_in, queries, keys, values = project(hidden, weights, tables, sizes)
    attended, stats = attention_forward(queries, keys, values, penalties)
    mlp_in, activated, slope, partial, partial_low = branches(hidden, attended, weights, sizes)
    kept = (hidden, attn_in, mlp_in, queries, keys, values, stats, attended, activated, slope)
    return partial, partial_low, kept


def layer_backward(low, weights, kept, tables, penalties, sizes, earlier, later_sum):
    last = earlier is not None
    hidden, attn_in, mlp_in, queries, keys, values, stats, attended, activated, slope = kept
    grad_attended, grad_upper, grad_mlp, mlp_sums, unit_sums = branches_back(
        low, slope, hidden, weights, sizes
    )
    terms = branch_terms(low, activated, mlp_in, grad_upper, attended, sizes)
    terms, grad_attended = lax.optimization_barrier((terms, grad_attended))
    if last:
        scatters = [Scatter(terms + earlier, sizes)]
        summed = later_sum
    else:
        scatters = []
        packed = jnp.concatenate([terms[0], sizes.pack_down(terms[1]), terms[2]], axis=1)
        packed, grad_attended = lax.optimization_barrier((packed, grad_attended))
        summed = lax.psum_scatter(packed, "seq", scatter_dimension=0, tiled=True)
    (grad_mixed,), _ = beside(
        scatters,
        (grad_attended,),
        lambda grads: (
            attention_backward(
                queries, keys, values, attended, grads, stats, tables, penalties
            ),
        ),
    )
    if last:
        later_sum, grad_mixed = lax.optimization_barrier((later_sum, grad_mixed))
    (partial, partial_low, attn_sums, mixed_sums), _ = beside(
        scatters,
        (grad_mixed,),
        lambda mixed: project_back(mixed, grad_mlp, hidden, weights, sizes),
    )
    grad_qkv, brought = beside(
        [],
        (grad_mixed,),
        lambda mixed: dot_tn(attn_in, mixed).astype(BF16),
        cp_sends(partial, partial_low, last),
    )
    sums = vector_sums(attn_sums, mlp_sums, mixed_sums, unit_sums, sizes)
    if last:
        summed = later_sum
        scatters.append(Scatter([grad_qkv], sizes))
    return cp_total(partial, brought, last), sums, summed, grad_qkv, scatters


def branch_terms(low, activated, mlp_in, grad_upper, attended, sizes):
    up = dot_tn(mlp_in, grad_upper).astype(BF16)
    down = dot_tn(activated, low).astype(BF16)
    dense = jnp.zeros((sizes.members * sizes.width, sizes.features), BF16)
    dense = lax.dynamic_update_slice_in_dim(
        dense, dot_tn(attended, low).astype(BF16), lax.axis_index("cp") * sizes.width, 0
    )
    return [up, down, dense[: sizes.features]]


def vector_sums(attn_sums, mlp_sums, qkv_bias, up_bias, sizes):
    me = lax.axis_index("cp")
    local, padded = sizes.width, sizes.members * sizes.width
    out_bias = jnp.where(me == 0, mlp_sums[2:3], 0.0)
    rows = [attn_sums[0:1], attn_sums[1:2], mlp_sums[0:1], mlp_sums[1:2], out_bias]
    for part in range(3):
        row = jnp.zeros((1, padded), F32)
        row = lax.dynamic_update_slice(
            row, qkv_bias[0:1, part * local : (part + 1) * local], (0, me * local)
        )
        rows.append(row[:, : HEADS * HEAD_DIM])
    up = jnp.zeros((1, sizes.members * sizes.hidden), F32)
    rows.append(lax.dynamic_update_slice(up, up_bias[0:1], (0, me * sizes.hidden)))
    return jnp.concatenate(rows, axis=1)


def finish_gradients(summed, sizes):
    members, features, hidden, width = sizes.members, sizes.features, sizes.hidden, sizes.width
    rows = summed.shape[0] // members
    down = sizes.unpack_down(summed[:, hidden : 2 * hidden]).astype(BF16)
    down = to_users(down, sizes, back=True).astype(F32)
    joined = jnp.concatenate([summed[:, :hidden], summed[:, 2 * hidden :]], axis=1)
    joined = cp_exchange(joined.reshape(members, rows, -1))
    up = jnp.transpose(joined[:, :, :hidden], (1, 0, 2)).reshape(rows, -1)
    dense = jnp.sum(joined[:, :, hidden : hidden + features], axis=0)
    qkv = joined[:, :, hidden + features :].reshape(members, rows, 3, width)
    qkv = jnp.transpose(qkv, (1, 2, 0, 3)).reshape(rows, 3, members * width)
    qkv = qkv[:, :, : HEADS * HEAD_DIM].reshape(rows, -1)
    return qkv, dense, up, down


def per_device(inputs, doc_ids, cotangent, *params):
    sizes = Sizes(inputs.shape[1], params[8].shape[2])
    small = (0, 1, 2, 3, 5, 7, 9, 11)
    docs = cp_gather(doc_ids)
    exchanged, docs, inputs, cotangent, vectors = lax.optimization_barrier(
        (
            cp_exchange(cut_columns(params, sizes)), docs, inputs, cotangent,
            [params[index] for index in small],
        )
    )
    params = list(params)
    for index, vector in zip(small, vectors):
        params[index] = vector
    tokens = jnp.stack([inputs, cotangent])
    if sizes.members == 2:
        fetched, other = fetch_layers(
            params, exchanged, to_users(params[10], sizes), sizes, cp_peer(tokens)
        )
        first = lax.axis_index("cp") == 0
        both = jnp.stack([jnp.where(first, tokens, other), jnp.where(first, other, tokens)])
    else:
        fetched, tokens = fetch_layers(
            params, exchanged, to_users(params[10], sizes), sizes, tokens
        )
        both = cp_gather(tokens[None])
    vectors = fetch_vectors(params, sizes)
    for layer in range(LAYERS):
        fetched[layer].update(vectors[layer])
    both = both.astype(F32)
    hidden = both[:, 0].reshape(-1, inputs.shape[1])
    low = both[:, 1].reshape(-1, inputs.shape[1]).astype(BF16)
    place = jnp.arange(docs.shape[0], dtype=jnp.int32)
    starts = jnp.sum((docs[None, :] < docs[:, None]).astype(jnp.int32), axis=1)
    tables = rotary_tables(place - starts)
    penalties = document_penalties(docs)
    me = lax.axis_index("cp")
    rows = inputs.shape[0]

    def own_rows(array):
        return lax.dynamic_slice_in_dim(array, me * rows, rows, 0)

    records = []
    for layer in range(LAYERS):
        partial, partial_low, kept = layer_forward(
            hidden, fetched[layer], tables, penalties, sizes
        )
        records.append(kept)
        out_bias = fetched[layer]["out_bias"]
        if layer < LAYERS - 1:
            hidden = hidden + cp_sum(partial, partial_low) + out_bias
        else:
            output = own_rows(hidden) + cp_sum_rows(partial, partial_low) + out_bias
    vector_terms, summed, earlier, layer_sum = [], [], None, None
    upstream = low.astype(F32)
    for layer in reversed(range(LAYERS)):
        total, sums, layer_sum, grad_qkv, scatters = layer_backward(
            low, fetched[layer], records[layer], tables, penalties, sizes, earlier, layer_sum
        )
        vector_terms.append(sums)
        if layer == 0:
            summed[-1:] = [layer_sum]
        else:
            summed.append(layer_sum)
        if layer > 0:
            earlier = (earlier or []) + [grad_qkv]
            upstream = upstream + total
            low = upstream.astype(BF16)
        else:
            input_grad = own_rows(upstream) + total
    flat = sum_everywhere(jnp.concatenate(vector_terms[::-1]))
    finish(scatters)
    mixed, last_qkv = scatters[0].result, scatters[1].result
    first = 2 * sizes.hidden + sizes.features
    width = 3 * sizes.width
    sums = [jnp.concatenate([mixed[:, :first], last_qkv], axis=1)] + [
        jnp.concatenate(
            [
                summed[index].astype(F32),
                mixed[:, first + index * width : first + (index + 1) * width],
            ],
            axis=1,
        )
        for index in range(LAYERS - 1)
    ][::-1]
    qkv, dense, up, down = (
        jnp.stack(grads) for grads in zip(*(finish_gradients(part, sizes) for part in sums))
    )
    owner, features = lax.axis_index("seq") * sizes.members + me, sizes.features
    own, first = [], 0
    for blocks in (1, 1, 1, 1, 1, 3, sizes.ratio):
        share = blocks * sizes.owned
        own.append(lax.dynamic_slice_in_dim(flat, first + owner * share, share, 1))
        first += blocks * features
    gain_attn, bias_attn, gain_mlp, bias_mlp, out_bias, qkv_bias, up_bias = own
    return (
        output.astype(BF16), input_grad, gain_attn, bias_attn, gain_mlp, bias_mlp, qkv, qkv_bias,
        dense, out_bias, up, up_bias, down, out_bias,
    )


def solution(mesh):
    rows, shared = P(("seq", "cp")), P(None, ("seq", "cp"))
    return jax.shard_map(
        per_device,
        mesh=mesh,
        in_specs=(rows,) * 3 + (shared,) * 12,
        out_specs=(rows,) * 2 + (shared,) * 12,
        check_vma=False,
    )
```

```python
import functools

import jax
import jax.numpy as jnp
from jax import lax
from jax.experimental import pallas as pl
from jax.experimental.pallas import tpu as pltpu
from jax.sharding import PartitionSpec as P

HEADS = 12
HEAD_DIM = 64
ROT_DIM = 16
LAYERS = 2
LANES = 128
Q_BLOCK = 256

EPSILON = 1e-05
MASKED = -1e30
F32 = jnp.float32
BF16 = jnp.bfloat16
VMEM_LIMIT = 48 * 1024 * 1024


def pick(array, index, axis=0):
    return lax.dynamic_index_in_dim(array, index, axis, keepdims=False)


def dot_nn(left, right):
    return lax.dot_general(left, right, (((1,), (0,)), ((), ())), preferred_element_type=F32)


def dot_nt(left, right):
    return lax.dot_general(left, right, (((1,), (1,)), ((), ())), preferred_element_type=F32)


def dot_tn(left, right):
    return lax.dot_general(left, right, (((0,), (0,)), ((), ())), preferred_element_type=F32)


def cp_peer(array):
    return lax.ppermute(array, "cp", [(0, 1), (1, 0)])


def cp_gather(array):
    if lax.axis_size("cp") != 2:
        return lax.all_gather(array, "cp", axis=0, tiled=True)
    other = cp_peer(array)
    first = lax.axis_index("cp") == 0
    return jnp.concatenate([jnp.where(first, array, other), jnp.where(first, other, array)])


def cp_exchange(blocks):
    if lax.axis_size("cp") != 2:
        return lax.all_to_all(blocks, "cp", 0, 0)
    me = lax.axis_index("cp")
    mine = pick(blocks, me)
    other = cp_peer(pick(blocks, 1 - me).astype(BF16)).astype(blocks.dtype)
    first = me == 0
    return jnp.stack([jnp.where(first, mine, other), jnp.where(first, other, mine)])


def cp_sum(partial, low):
    if lax.axis_size("cp") != 2:
        return lax.psum(partial, "cp")
    return partial + cp_peer(low).astype(F32)


def cp_sends(partial, low, own_rows):
    if lax.axis_size("cp") != 2:
        if own_rows:
            return [(partial, lambda a: lax.psum_scatter(a, "cp", scatter_dimension=0, tiled=True))]
        return [(partial, lambda a: lax.psum(a, "cp"))]
    if own_rows:
        rows = partial.shape[0] // 2
        other = (1 - lax.axis_index("cp")) * rows
        low = lax.dynamic_slice_in_dim(low, other, rows, 0)
    return [(low, cp_peer)]


def cp_total(partial, brought, own_rows):
    if lax.axis_size("cp") != 2:
        return brought[0]
    if own_rows:
        rows = partial.shape[0] // 2
        partial = lax.dynamic_slice_in_dim(partial, lax.axis_index("cp") * rows, rows, 0)
    return partial + brought[0].astype(F32)


def cp_sum_rows(partial, low):
    if lax.axis_size("cp") != 2:
        return lax.psum_scatter(partial, "cp", scatter_dimension=0, tiled=True)
    rows = partial.shape[0] // 2
    me = lax.axis_index("cp")
    other = cp_peer(lax.dynamic_slice_in_dim(low, (1 - me) * rows, rows, 0))
    return lax.dynamic_slice_in_dim(partial, me * rows, rows, 0) + other.astype(F32)


def seq_shift(array, target):
    count = lax.axis_size("seq")
    return lax.ppermute(array, "seq", [(i, target(i) % count) for i in range(count)])


def ring_next(array):
    return seq_shift(array, lambda i: i + 4)


def pair_swap(array):
    return seq_shift(array, lambda i: i ^ 2)


def core_swap(array):
    return seq_shift(array, lambda i: i ^ 1)


def sum_everywhere(array):
    count = lax.axis_size("seq")
    if lax.axis_size("cp") != 2 or count & (count - 1):
        return lax.psum(array, ("seq", "cp"))
    array = array + cp_peer(array)
    bit = 1
    while bit < count:
        array = array + seq_shift(array, lambda i, bit=bit: i ^ bit)
        bit *= 2
    return array


def seq_place():
    me = lax.axis_index("seq")
    return me // 4, (me // 2) % 2, me % 2


def seq_gather(block, later):
    count = lax.axis_size("seq")
    if count % 8:
        return lax.all_gather(block, "seq", axis=0, tiled=True), later
    rings = count // 4
    ring, pair, core = seq_place()
    result = jnp.zeros((rings, 2, 2) + block.shape, block.dtype)
    held, waiting = block, []
    for step in range(rings):
        following = ring_next(held) if step < rings - 1 else None
        other = pair_swap(held)
        waiting.append(
            jnp.where(pair == 0, jnp.stack([held, other]), jnp.stack([other, held]))
        )
        held = following
        if step == rings - 2:
            held, later = lax.optimization_barrier((held, later))
        if step % 2 == 0:
            continue
        both = jnp.stack(waiting)
        sibling = core_swap(both)
        quads = jnp.where(
            core == 0, jnp.stack([both, sibling], axis=2), jnp.stack([sibling, both], axis=2)
        )
        for index in range(2):
            result = lax.dynamic_update_slice(
                result,
                quads[index : index + 1],
                ((ring - step + 1 - index) % rings,) + (0,) * (quads.ndim - 1),
            )
        waiting = []
    return result.reshape((count * block.shape[0],) + block.shape[1:]), later


def turn(block, cosine, sine_up, sine_down):
    return (
        block * cosine
        + pltpu.roll(block, LANES - ROT_DIM // 2, 1) * sine_up
        + pltpu.roll(block, ROT_DIM // 2, 1) * sine_down
    )


def turn_back(block, cosine, sine_up, sine_down):
    return (
        block * cosine
        + pltpu.roll(block * sine_up, ROT_DIM // 2, 1)
        + pltpu.roll(block * sine_down, LANES - ROT_DIM // 2, 1)
    )


def head_lanes(shape, head):
    lane = lax.broadcasted_iota(jnp.int32, shape, 1)
    return (lane < HEAD_DIM) if head == 0 else (lane >= HEAD_DIM)


def keys_first(rows):
    key_place = lax.broadcasted_iota(jnp.int32, (rows, rows), 0)
    query_place = lax.broadcasted_iota(jnp.int32, (rows, rows), 1)
    return key_place <= query_place


def forward_kernel(
    q_ref, k_ref, v_ref, query_pen, key_pen, out_ref, stat_ref, turned_t,
):
    rows = q_ref.shape[0]
    queries, keys, values = q_ref[...], k_ref[...], v_ref[...]
    value_t = values.astype(F32).T.astype(BF16)
    block = min(Q_BLOCK, rows)
    causal = keys_first(block)
    for head in range(2):
        lanes = head_lanes((rows, LANES), head)
        head_q = jnp.where(lanes, queries, query_pen[...])
        head_k = jnp.where(lanes, keys, key_pen[...])
        head_v = value_t[head * HEAD_DIM : (head + 1) * HEAD_DIM, :]
        for start in range(0, rows, block):
            stop = start + block
            scores = dot_nt(head_k[:stop], head_q[start:stop])
            last = jnp.where(causal, scores[start:], MASKED)
            scores = last if start == 0 else jnp.concatenate([scores[:start], last])
            top = jnp.max(scores, axis=0, keepdims=True)
            terms = jnp.exp(scores - top)
            total = jnp.sum(terms, axis=0, keepdims=True)
            summed = dot_nn(head_v[:, :stop], terms.astype(BF16))
            turned_t[head * HEAD_DIM : (head + 1) * HEAD_DIM, start:stop] = summed / total
            stat_ref[0, head : head + 1, start:stop] = top + jnp.log(total)
    out_ref[...] = turned_t[...].T.astype(BF16)


def attention_forward(queries, keys, values, penalties):
    rows, width = queries.shape
    pairs = width // LANES
    whole = pl.BlockSpec((rows, LANES), lambda p: (0, 0))
    column = pl.BlockSpec((rows, LANES), lambda p: (0, p))
    return pl.pallas_call(
        forward_kernel,
        grid=(pairs,),
        in_specs=[column] * 3 + [whole] * 2,
        out_specs=[column, pl.BlockSpec((1, 2, rows), lambda p: (p, 0, 0))],
        out_shape=[
            jax.ShapeDtypeStruct((rows, width), BF16),
            jax.ShapeDtypeStruct((pairs, 2, rows), F32),
        ],
        scratch_shapes=[pltpu.VMEM((LANES, rows), F32)],
        compiler_params=pltpu.CompilerParams(vmem_limit_bytes=VMEM_LIMIT),
        cost_estimate=pl.CostEstimate(
            flops=pairs * rows * rows * LANES,
            bytes_accessed=rows * width,
            transcendentals=0,
        ),
        name="attention_forward",
    )(queries, keys, values, *penalties)


def backward_kernel(
    q_ref, k_ref, v_ref, out_ref, grad_ref, stat_ref, cos_ref, up_ref, down_ref, query_pen, key_pen,
    mixed_ref, delta_t, grad_q,
):
    rows = q_ref.shape[0]
    width = mixed_ref.shape[1] // 3
    pair = pl.program_id(0)
    queries, keys, values, grads = q_ref[...], k_ref[...], v_ref[...], grad_ref[...]
    products = (grads.astype(F32) * out_ref[...].astype(F32)).T
    for head in range(2):
        delta_t[head : head + 1, :] = jnp.sum(
            products[head * HEAD_DIM : (head + 1) * HEAD_DIM, :], axis=0, keepdims=True
        )
    tables = (cos_ref[...], up_ref[...], down_ref[...])
    grad_q[...] = jnp.zeros_like(grad_q)
    block = min(Q_BLOCK, rows)
    causal = keys_first(block)
    none = jnp.zeros((rows, LANES), BF16)
    heads = []
    for head in range(2):
        lanes = head_lanes((rows, LANES), head)
        heads.append(
            (
                jnp.where(lanes, queries, query_pen[...]),
                jnp.where(lanes, keys, key_pen[...]),
                jnp.where(lanes, queries, none),
                jnp.where(lanes, keys, none),
                jnp.where(lanes, values, none),
                jnp.where(lanes, grads, none),
            )
        )
    for start in range(0, rows, block):
        stop = start + block
        grad_k, grad_v = None, None
        for head, (score_q, score_k, head_q, head_k, head_v, head_g) in enumerate(heads):
            scores = dot_nt(score_k[start:stop], score_q[start:])
            first = jnp.where(causal, scores[:, :block], MASKED)
            scores = (
                first if stop == rows else jnp.concatenate([first, scores[:, block:]], axis=1)
            )
            weights = jnp.exp(scores - stat_ref[0, head : head + 1, start:])
            grad_p = dot_nt(head_v[start:stop], head_g[start:])
            grad_s = (weights * (grad_p - delta_t[head : head + 1, start:])).astype(BF16)
            more_v = dot_nn(weights.astype(BF16), head_g[start:])
            more_k = dot_nn(grad_s, head_q[start:])
            grad_v = more_v if grad_v is None else grad_v + more_v
            grad_k = more_k if grad_k is None else grad_k + more_k
            grad_q[start:, :] += dot_tn(grad_s, head_k[start:stop])
        block_tables = tuple(table[start:stop] for table in tables)
        mixed_ref[start:stop, pl.ds(pl.multiple_of(width + pair * LANES, LANES), LANES)] = (
            turn_back(grad_k, *block_tables).astype(BF16)
        )
        mixed_ref[start:stop, pl.ds(pl.multiple_of(2 * width + pair * LANES, LANES), LANES)] = (
            grad_v.astype(BF16)
        )
    mixed_ref[:, pl.ds(pl.multiple_of(pair * LANES, LANES), LANES)] = turn_back(
        grad_q[...] * HEAD_DIM**-0.5, *tables
    ).astype(BF16)


def attention_backward(queries, keys, values, attended, grad_attended, stats, tables, penalties):
    rows, width = queries.shape
    pairs = width // LANES
    whole = pl.BlockSpec((rows, LANES), lambda p: (0, 0))
    column = pl.BlockSpec((rows, LANES), lambda p: (0, p))
    stat = pl.BlockSpec((1, 2, rows), lambda p: (p, 0, 0))
    return pl.pallas_call(
        backward_kernel,
        grid=(pairs,),
        in_specs=[column] * 5 + [stat] + [whole] * 5,
        out_specs=pl.BlockSpec((rows, 3 * width), lambda p: (0, 0)),
        out_shape=jax.ShapeDtypeStruct((rows, 3 * width), BF16),
        scratch_shapes=[pltpu.VMEM((2, rows), F32), pltpu.VMEM((rows, LANES), F32)],
        compiler_params=pltpu.CompilerParams(vmem_limit_bytes=VMEM_LIMIT),
        cost_estimate=pl.CostEstimate(
            flops=pairs * rows * rows * LANES,
            bytes_accessed=rows * width,
            transcendentals=0,
        ),
        name="attention_backward",
    )(queries, keys, values, attended, grad_attended, stats, *tables, *penalties)


ROW_BLOCK = 256


def layer_norm(hidden):
    average = jnp.mean(hidden, axis=-1, keepdims=True)
    centered = hidden - average
    variance = jnp.mean(centered * centered, axis=-1, keepdims=True)
    inverse_std = lax.rsqrt(variance + EPSILON)
    return centered * inverse_std, inverse_std


def load_parts(parts, semaphores):
    copies = [
        pltpu.make_async_copy(source, target, semaphores.at[index])
        for index, (source, target) in enumerate(parts)
    ]
    first = pl.program_id(0) == 0

    @pl.when(first)
    def _():
        for copy in copies:
            copy.start()

    def wait(*indices):
        @pl.when(first)
        def _():
            for index in indices:
                copies[index].wait()

    return wait


def down_parts(source, sizes, target):
    if sizes.slabs == 0:
        return [(source, target)]
    first, rows, features = sizes.split + sizes.hidden, sizes.rows, sizes.features
    parts = []
    for group in range(sizes.groups):
        for slab in range(sizes.slabs):
            lanes = slice(first + slab * features, first + (slab + 1) * features)
            start = (group * sizes.slabs + slab) * rows
            parts.append(
                (
                    source.at[group * rows : (group + 1) * rows, lanes],
                    target.at[start : start + rows, :],
                )
            )
    return parts


def project_kernel(
    sizes, hidden, gain, bias, qkv_bias, whole, cos_ref, up_ref, down_ref,
    attn_in, q_ref, k_ref, v_ref, qkv, semaphores,
):
    width = sizes.width
    wait = load_parts([(whole.at[:, : 3 * width], qkv)], semaphores)
    normed, _ = layer_norm(hidden[...])
    low = (normed * gain[...] + bias[...]).astype(BF16)
    attn_in[...] = low
    wait(0)
    tables = (cos_ref[...], up_ref[...], down_ref[...])
    mixed = dot_nn(low, qkv[...]) + qkv_bias[...]
    for start in range(0, width, LANES):
        lanes = slice(start, start + LANES)
        turned = turn(mixed[:, start : start + LANES], *tables).astype(BF16)
        q_ref[:, lanes] = turned * jnp.asarray(HEAD_DIM**-0.5, BF16)
        first = width + start
        k_ref[:, lanes] = turn(mixed[:, first : first + LANES], *tables).astype(BF16)
    v_ref[...] = mixed[:, 2 * width :].astype(BF16)


def row_call(kernel, sizes, rows, operands, results, scratch, copies, flops, name):
    block = min(ROW_BLOCK, rows)

    def spec(shape, kind):
        if kind == "hbm":
            return pl.BlockSpec(memory_space=pl.ANY)
        if kind == "rows":
            return pl.BlockSpec((block, shape[1]), lambda i: (i, 0))
        return pl.BlockSpec(shape, lambda i: (0, 0))

    return pl.pallas_call(
        functools.partial(kernel, sizes),
        grid=(rows // block,),
        in_specs=[spec(array.shape, kind) for array, kind in operands],
        out_specs=[spec(shape, kind) for shape, _, kind in results],
        out_shape=[jax.ShapeDtypeStruct(shape, dtype) for shape, dtype, _ in results],
        scratch_shapes=scratch + [pltpu.SemaphoreType.DMA((copies,))],
        compiler_params=pltpu.CompilerParams(vmem_limit_bytes=VMEM_LIMIT),
        cost_estimate=pl.CostEstimate(
            flops=flops // 8, bytes_accessed=rows * sizes.features, transcendentals=0
        ),
        name=name,
    )(*[array for array, _ in operands])


def project(hidden, weights, tables, sizes):
    rows, features, width = hidden.shape[0], sizes.features, sizes.width
    return row_call(
        project_kernel, sizes, rows,
        [(hidden, "rows"), (weights["gain_attn"], "all"), (weights["bias_attn"], "all"),
         (weights["qkv_bias"], "all"), (weights["whole"], "hbm")]
        + [(table, "rows") for table in tables],
        [((rows, features), BF16, "rows")] + [((rows, width), BF16, "rows")] * 3,
        [pltpu.VMEM((features, 3 * width), BF16)], 1,
        2 * rows * features * 3 * width, "project",
    )


ERFC_TERMS = (
    0.17087277, -0.82215223, 1.48851587, -1.13520398, 0.27886807,
    -0.18628806, 0.09678418, 0.37409196, 1.00002368, -1.26551223,
)


def gelu_and_slope(upper):
    size = jnp.abs(upper) * 0.5**0.5
    inverse = 1.0 / (1.0 + 0.5 * size)
    series = inverse * ERFC_TERMS[0] + ERFC_TERMS[1]
    for term in ERFC_TERMS[2:]:
        series = series * inverse + term
    square = size * size
    tail = 0.5 * inverse * jnp.exp(series - square)
    below = jnp.where(upper < 0, tail, 1.0 - tail)
    slope = below + upper * (jnp.exp(-square) * 0.3989422804014327)
    return upper * below, slope


def branches_kernel(
    sizes, hidden, attended, gain, bias, up_bias, whole, down_source, dense,
    mlp_in, activated, slope_ref, partial, partial_low, up, down, semaphores,
):
    up_part = (whole.at[:, sizes.split : sizes.split + sizes.hidden], up)
    downs = down_parts(down_source, sizes, down)
    wait = load_parts([up_part] + downs, semaphores)
    normed, _ = layer_norm(hidden[...])
    low = (normed * gain[...] + bias[...]).astype(BF16)
    mlp_in[...] = low
    total = dot_nn(attended[...], dense[...])
    wait(0)
    act, slope = gelu_and_slope(dot_nn(low, up[...]) + up_bias[...])
    act = act.astype(BF16)
    activated[...] = act
    slope_ref[...] = slope.astype(BF16)
    wait(*range(1, 1 + len(downs)))
    total = total + dot_nn(act, down[...])
    partial[...] = total
    partial_low[...] = total.astype(BF16)


def branches(hidden, attended, weights, sizes):
    rows, features, units, width = hidden.shape[0], sizes.features, sizes.hidden, sizes.width
    return row_call(
        branches_kernel, sizes, rows,
        [(hidden, "rows"), (attended, "rows"), (weights["gain_mlp"], "all"),
         (weights["bias_mlp"], "all"), (weights["up_bias"], "all"), (weights["whole"], "hbm"),
         (weights["down"], "hbm"), (weights["dense"], "all")],
        [((rows, features), BF16, "rows")] + [((rows, units), BF16, "rows")] * 2
        + [((rows, features), F32, "rows"), ((rows, features), BF16, "rows")],
        [pltpu.VMEM((features, units), BF16), pltpu.VMEM((units, features), BF16)],
        1 + sizes.down_copies, 2 * rows * features * (2 * units + width), "branches",
    )


def add_sums(ref, index, block):
    ref[index : index + 1, :] += jnp.sum(block, axis=0, keepdims=True)


def branches_back_kernel(
    sizes, low_ref, slope, hidden, gain, whole, down_source, dense,
    grad_attended, grad_upper, grad_mlp, sums, unit_sums, up, down, semaphores,
):
    downs = down_parts(down_source, sizes, down)
    up_part = (whole.at[:, sizes.split : sizes.split + sizes.hidden], up)
    wait = load_parts(downs + [up_part], semaphores)

    @pl.when(pl.program_id(0) == 0)
    def _():
        sums[...] = jnp.zeros_like(sums)
        unit_sums[...] = jnp.zeros_like(unit_sums)

    low = low_ref[...]
    grad_attended[...] = dot_nt(low, dense[...]).astype(BF16)
    normed, _ = layer_norm(hidden[...])
    wait(*range(len(downs)))
    upper = (dot_nt(low, down[...]) * slope[...].astype(F32)).astype(BF16)
    grad_upper[...] = upper
    add_sums(unit_sums, 0, upper.astype(F32))
    wait(len(downs))
    grad = dot_nt(upper, up[...])
    add_sums(sums, 0, grad * normed)
    add_sums(sums, 1, grad)
    add_sums(sums, 2, low.astype(F32))
    grad_mlp[...] = grad * gain[...]


def branches_back(low, slope, hidden, weights, sizes):
    rows, features, units, width = hidden.shape[0], sizes.features, sizes.hidden, sizes.width
    return row_call(
        branches_back_kernel, sizes, rows,
        [(low, "rows"), (slope, "rows"), (hidden, "rows"), (weights["gain_mlp"], "all"),
         (weights["whole"], "hbm"), (weights["down"], "hbm"), (weights["dense"], "all")],
        [((rows, width), BF16, "rows"), ((rows, units), BF16, "rows"),
         ((rows, features), F32, "rows"), ((8, features), F32, "all"), ((8, units), F32, "all")],
        [pltpu.VMEM((features, units), BF16), pltpu.VMEM((units, features), BF16)],
        1 + sizes.down_copies, 2 * rows * features * (2 * units + width), "branches_back",
    )


def project_back_kernel(
    sizes, mixed, grad_mlp, hidden, gain, whole, partial, partial_low, sums, mixed_sums, qkv,
    semaphores,
):
    wait = load_parts([(whole.at[:, : 3 * sizes.width], qkv)], semaphores)

    @pl.when(pl.program_id(0) == 0)
    def _():
        sums[...] = jnp.zeros_like(sums)
        mixed_sums[...] = jnp.zeros_like(mixed_sums)

    normed, inverse_std = layer_norm(hidden[...])
    add_sums(mixed_sums, 0, mixed[...].astype(F32))
    wait(0)
    grad = dot_nt(mixed[...], qkv[...])
    add_sums(sums, 0, grad * normed)
    add_sums(sums, 1, grad)
    grad = grad * gain[...] + grad_mlp[...]
    centered = (
        grad
        - jnp.mean(grad, axis=-1, keepdims=True)
        - normed * jnp.mean(grad * normed, axis=-1, keepdims=True)
    )
    grad = inverse_std * centered
    partial[...] = grad
    partial_low[...] = grad.astype(BF16)


def project_back(grad_mixed, grad_mlp, hidden, weights, sizes):
    rows, features, width = hidden.shape[0], sizes.features, sizes.width
    return row_call(
        project_back_kernel, sizes, rows,
        [(grad_mixed, "rows"), (grad_mlp, "rows"), (hidden, "rows"),
         (weights["gain_attn"], "all"), (weights["whole"], "hbm")],
        [((rows, features), F32, "rows"), ((rows, features), BF16, "rows"),
         ((8, features), F32, "all"), ((8, 3 * width), F32, "all")],
        [pltpu.VMEM((features, 3 * width), BF16)], 1,
        2 * rows * features * 3 * width, "project_back",
    )


def lay_out(refs, widths, sizes, store):
    first = 0
    for ref, width in zip(refs, widths):
        if width is None:
            for slab in range(sizes.slabs):
                rows = slice(slab * sizes.rows, (slab + 1) * sizes.rows)
                store(ref[rows, :], slice(first, first + sizes.features))
                first += sizes.features
        else:
            store(ref[...], slice(first, first + width))
            first += width


def pack_kernel(sizes, widths, place, *refs):
    packed = refs[-1]

    def store(block, lanes):
        packed[0, 0, :, lanes] = block

    lay_out(refs[:-1], widths, sizes, store)


def first_sum_kernel(sizes, widths, place, *refs):
    count = len(widths)
    sibling_sent, sibling_mine, sent, mine = refs[2 * count :]

    def store_sent(block, lanes):
        total = block.astype(F32) + sibling_sent[0, 0, :, lanes].astype(F32)
        sent[0, :, lanes] = total.astype(BF16)

    def store_mine(block, lanes):
        mine[0, :, lanes] = block.astype(F32) + sibling_mine[0, 0, :, lanes].astype(F32)

    lay_out(refs[:count], widths, sizes, store_sent)
    lay_out(refs[count : 2 * count], widths, sizes, store_mine)


class Scatter:
    def __init__(self, parts, sizes):
        self.sizes, self.stage, self.operands, self.result = sizes, 0, [], None
        self.rings = sizes.groups // 4
        self.kernels = sizes.groups % 8 == 0 and sizes.rows % 16 == 0
        self.parts = [
            part if owned else (part if part.shape[0] == sizes.features else sizes.pack_down(part))
            for part, owned in ((part, self.kernels) for part in parts)
        ]
        self.widths = [
            part.shape[1] if part.shape[0] == sizes.features else None for part in self.parts
        ]
        self.columns = sum(part.size for part in self.parts) // sizes.features
        if not self.kernels:
            packed = jnp.concatenate(self.parts, axis=1)
            summed = lax.psum_scatter(packed, "seq", scatter_dimension=0, tiled=True)
            self.result = summed.astype(F32)
            return
        ring, pair, core = seq_place()
        self.place = jnp.stack([ring, pair, core]).astype(jnp.int32)
        self.operands = [self.pack()]

    def cost(self):
        return pl.CostEstimate(
            flops=0, bytes_accessed=self.sizes.features * self.columns * 4, transcendentals=0
        )

    def specs(self, index):
        rows = self.sizes.rows
        return [
            pl.BlockSpec((rows * (self.sizes.slabs if width is None else 1), part.shape[1]), index)
            for part, width in zip(self.parts, self.widths)
        ]

    def pack(self):
        def other(ring, pair, place):
            return ((ring * 2 + pair) * 2 + 1 - place[2], 0)

        rows, rings = self.sizes.rows, self.rings
        return pl.pallas_call(
            functools.partial(pack_kernel, self.sizes, self.widths),
            grid_spec=pltpu.PrefetchScalarGridSpec(
                num_scalar_prefetch=1,
                grid=(rings, 2),
                in_specs=self.specs(other),
                out_specs=pl.BlockSpec((1, 1, rows, self.columns), lambda r, p, place: (r, p, 0, 0)),
            ),
            out_shape=jax.ShapeDtypeStruct((rings, 2, rows, self.columns), BF16),
            compiler_params=pltpu.CompilerParams(vmem_limit_bytes=VMEM_LIMIT),
            cost_estimate=self.cost(),
            name="pack_terms",
        )(self.place, *self.parts)

    def first_sum(self):
        rows, rings, columns = self.sizes.rows, self.rings, self.columns

        def ring_of(step, place):
            return lax.rem(place[0] + 2 * rings - 1 - step, rings)

        def own(pair_of):
            return lambda step, place: (
                (ring_of(step, place) * 2 + pair_of(place)) * 2 + place[2],
                0,
            )

        def sibling(pair_of):
            return pl.BlockSpec(
                (1, 1, rows, columns),
                lambda step, place: (ring_of(step, place), pair_of(place), 0, 0),
            )

        def away(place):
            return 1 - place[1]

        def home(place):
            return place[1]

        step_block = pl.BlockSpec((1, rows, columns), lambda step, place: (step, 0, 0))
        return pl.pallas_call(
            functools.partial(first_sum_kernel, self.sizes, self.widths),
            grid_spec=pltpu.PrefetchScalarGridSpec(
                num_scalar_prefetch=1,
                grid=(rings,),
                in_specs=self.specs(own(away))
                + self.specs(own(home))
                + [sibling(away), sibling(home)],
                out_specs=[step_block, step_block],
            ),
            out_shape=[
                jax.ShapeDtypeStruct((rings, rows, columns), BF16),
                jax.ShapeDtypeStruct((rings, rows, columns), F32),
            ],
            compiler_params=pltpu.CompilerParams(vmem_limit_bytes=VMEM_LIMIT),
            cost_estimate=self.cost(),
            name="first_sum",
        )(self.place, *self.parts, *self.parts, self.sibling, self.sibling)

    def launch(self, operands):
        if self.stage == 0:
            return [core_swap(operands[0])]
        if self.stage == 1:
            self.arrived = [pair_swap(operand) for operand in operands]
            return self.arrived[:1]
        return [ring_next(operands[0])]

    def land(self, received):
        if self.stage == 0:
            self.sibling = received[0]
        elif self.stage == 1:
            self.arrived[0] = received[0]
        else:
            self.received = received[0]
        self.stage += 1

    def prepare(self):
        if self.result is not None or self.stage == 0:
            return
        half = self.rings // 2
        if self.stage == 1:
            sent, self.mine = self.first_sum()
            self.operands = [sent[:half], sent[half:]]
            return
        step = self.stage - 2
        total = self.mine[step] + self.arrived[step // half][step % half].astype(F32)
        if step > 0:
            total = total + self.received.astype(F32)
        if step == self.rings - 1:
            self.result, self.operands = total, []
        else:
            self.operands = [total.astype(BF16)]


def beside(scatters, inputs, compute, sends=()):
    scatters = [scatter for scatter in scatters if scatter.result is None]
    for scatter in scatters:
        scatter.prepare()
    scatters = [scatter for scatter in scatters if scatter.result is None]
    operands = [scatter.operands for scatter in scatters]
    inputs, operands, sent = lax.optimization_barrier(
        (tuple(inputs), operands, [operand for operand, _ in sends])
    )
    landing = [scatter.launch(operand) for scatter, operand in zip(scatters, operands)]
    brought = [transfer(operand) for operand, (_, transfer) in zip(sent, sends)]
    short = [scatter.stage == 0 for scatter in scatters]
    tied = [received for received, is_short in zip(landing, short) if is_short]
    results, tied, brought = lax.optimization_barrier((compute(*inputs), tied, brought))
    for scatter, received, is_short in zip(scatters, landing, short):
        scatter.land(tied.pop(0) if is_short else received)
    return results, brought


def finish(scatters):
    while any(scatter.result is None for scatter in scatters):
        for scatter in scatters:
            if scatter.result is None:
                scatter.prepare()
            if scatter.result is None:
                scatter.land(scatter.launch(scatter.operands))


def rotary_tables(positions):
    half_rot = ROT_DIM // 2
    inverse = 10000.0 ** (-(jnp.arange(half_rot, dtype=F32) * 2.0 / ROT_DIM))
    angles = positions.astype(F32)[:, None] * inverse[None, :]
    cosine, sine = jnp.cos(angles), jnp.sin(angles)
    rows = positions.shape[0]
    rest = HEAD_DIM - ROT_DIM
    zeros = jnp.zeros_like(sine)
    still = jnp.zeros((rows, rest), F32)
    cosine = jnp.concatenate([cosine, cosine, jnp.ones((rows, rest), F32)] * 2, axis=1)
    sine_up = jnp.concatenate([-sine, zeros, still] * 2, axis=1)
    sine_down = jnp.concatenate([zeros, sine, still] * 2, axis=1)
    return cosine, sine_up, sine_down


def document_penalties(docs):
    slots = jnp.arange(LANES, dtype=jnp.int32) % HEAD_DIM
    same = docs[:, None] == slots[None, :]
    return jnp.where(same, 0.0, MASKED).astype(BF16), same.astype(BF16)


def pad_heads(array, axis, sizes):
    missing = sizes.members * sizes.width - HEADS * HEAD_DIM
    if missing == 0:
        return array
    pads = [(0, 0)] * array.ndim
    pads[axis] = (0, missing)
    return jnp.pad(array, pads)


class Sizes:
    def __init__(self, features, hidden):
        self.members, self.groups = lax.axis_size("cp"), lax.axis_size("seq")
        per_member = -(-HEADS // self.members)
        self.padded = self.members * (per_member + per_member % 2)
        self.width = self.padded // self.members * HEAD_DIM
        self.features = features
        self.rows = features // self.groups
        owned = hidden // (self.members * self.groups)
        self.slabs = owned // self.rows if owned % self.rows == 0 and self.rows % 16 == 0 else 0
        self.down_copies = max(self.slabs * self.groups, 1)
        self.hidden = hidden // self.members
        self.ratio = hidden // features
        self.split = 3 * self.width + features
        self.owned = features // (self.members * self.groups)

    def pack_down(self, rows):
        if self.slabs == 0:
            return rows.reshape(-1, self.hidden)
        rows = rows.reshape(-1, self.slabs, self.rows, self.features)
        return jnp.transpose(rows, (0, 2, 1, 3)).reshape(-1, self.hidden)

    def unpack_down(self, packed):
        if self.slabs == 0:
            return packed.reshape(-1, self.features)
        packed = packed.reshape(-1, self.rows, self.slabs, self.features)
        return jnp.transpose(packed, (0, 2, 1, 3)).reshape(-1, self.features)


def to_users(rows, sizes, back=False):
    count = sizes.members * sizes.groups
    moves = [(i, (i % sizes.groups) * sizes.members + i // sizes.groups) for i in range(count)]
    if back:
        moves = [(target, source) for source, target in moves]
    return lax.ppermute(rows, ("seq", "cp"), moves)


def cut_columns(params, sizes):
    qkv_weight, dense_weight, up_weight = params[4], params[6], params[8]
    layers, rows, members = qkv_weight.shape[0], qkv_weight.shape[1], sizes.members
    qkv = pad_heads(qkv_weight.reshape(layers, rows, 3, HEADS * HEAD_DIM), 3, sizes)
    shares = []
    for member in range(members):
        heads = slice(member * sizes.width, (member + 1) * sizes.width)
        units = slice(member * sizes.hidden, (member + 1) * sizes.hidden)
        shares.append(
            jnp.concatenate(
                [qkv[:, :, part, heads] for part in range(3)]
                + [dense_weight, up_weight[:, :, units]],
                axis=2,
            )
        )
    return jnp.stack(shares)


def fetch_layers(params, exchanged, down, sizes, tokens):
    packed = [
        jnp.concatenate(
            [
                exchanged[:, layer].reshape(-1, exchanged.shape[-1]),
                sizes.pack_down(down[layer]),
            ],
            axis=1,
        )
        for layer in range(LAYERS)
    ]
    first, later = seq_gather(packed[0], packed[1:] + [tokens])
    fetched = [unpack_layer(first, sizes)]
    for block in later[:-1]:
        whole = lax.all_gather(block, "seq", axis=0, tiled=True)
        fetched.append(unpack_layer(whole, sizes))
    return fetched, later[-1]


def fetch_vectors(params, sizes):
    vectors = [params[i] for i in (0, 1, 2, 3, 7, 11, 5, 9)]
    me = lax.axis_index("cp")
    owner = lax.axis_index("seq") * sizes.members + me
    layers = vectors[0].shape[0]
    placed = [
        lax.dynamic_update_slice(
            jnp.zeros((layers, vector.shape[1] * sizes.members * sizes.groups), BF16),
            vector,
            (0, owner * vector.shape[1]),
        )
        for vector in vectors
    ]
    widths = [vector.shape[1] for vector in placed]
    every = sum_everywhere(jnp.concatenate(placed, axis=1)).astype(F32)
    results = []
    for layer in range(layers):
        first, arrays = 0, []
        for width in widths:
            arrays.append(every[layer : layer + 1, first : first + width])
            first += width
        gain_attn, bias_attn, gain_mlp, bias_mlp, dense_bias, down_bias, qkv_bias, up_bias = arrays
        qkv_bias = pad_heads(qkv_bias.reshape(3, HEADS * HEAD_DIM), 1, sizes)
        qkv_bias = lax.dynamic_slice_in_dim(qkv_bias, me * sizes.width, sizes.width, 1)
        up_bias = lax.dynamic_slice_in_dim(up_bias, me * sizes.hidden, sizes.hidden, 1)
        results.append(
            {
                "qkv_bias": qkv_bias.reshape(1, -1), "up_bias": up_bias,
                "gain_attn": gain_attn, "bias_attn": bias_attn,
                "gain_mlp": gain_mlp, "bias_mlp": bias_mlp,
                "out_bias": dense_bias + down_bias,
            }
        )
    return results


def unpack_layer(whole, sizes):
    split, features = sizes.split, sizes.features
    dense = whole[:, 3 * sizes.width : split]
    down = whole if sizes.slabs else sizes.unpack_down(whole[:, split + sizes.hidden :])
    dense = jnp.pad(dense, ((0, sizes.members * sizes.width - features), (0, 0)))
    dense = lax.dynamic_slice_in_dim(
        dense, lax.axis_index("cp") * sizes.width, sizes.width, 0
    )
    return {"whole": whole, "dense": dense, "down": down}


def layer_forward(hidden, weights, tables, penalties, sizes):
    attn_in, queries, keys, values = project(hidden, weights, tables, sizes)
    attended, stats = attention_forward(queries, keys, values, penalties)
    mlp_in, activated, slope, partial, partial_low = branches(hidden, attended, weights, sizes)
    kept = (hidden, attn_in, mlp_in, queries, keys, values, stats, attended, activated, slope)
    return partial, partial_low, kept


def layer_backward(low, weights, kept, tables, penalties, sizes, earlier, later_sum):
    last = earlier is not None
    hidden, attn_in, mlp_in, queries, keys, values, stats, attended, activated, slope = kept
    grad_attended, grad_upper, grad_mlp, mlp_sums, unit_sums = branches_back(
        low, slope, hidden, weights, sizes
    )
    terms = branch_terms(low, activated, mlp_in, grad_upper, attended, sizes)
    terms, grad_attended = lax.optimization_barrier((terms, grad_attended))
    if last:
        scatters = [Scatter(terms + earlier, sizes)]
        summed = later_sum
    else:
        scatters = []
        packed = jnp.concatenate([terms[0], sizes.pack_down(terms[1]), terms[2]], axis=1)
        packed, grad_attended = lax.optimization_barrier((packed, grad_attended))
        summed = lax.psum_scatter(packed, "seq", scatter_dimension=0, tiled=True)
    (grad_mixed,), _ = beside(
        scatters,
        (grad_attended,),
        lambda grads: (
            attention_backward(
                queries, keys, values, attended, grads, stats, tables, penalties
            ),
        ),
    )
    if last:
        later_sum, grad_mixed = lax.optimization_barrier((later_sum, grad_mixed))
    (partial, partial_low, attn_sums, mixed_sums), _ = beside(
        scatters,
        (grad_mixed,),
        lambda mixed: project_back(mixed, grad_mlp, hidden, weights, sizes),
    )
    grad_qkv, brought = beside(
        [],
        (grad_mixed,),
        lambda mixed: dot_tn(attn_in, mixed).astype(BF16),
        cp_sends(partial, partial_low, last),
    )
    sums = vector_sums(attn_sums, mlp_sums, mixed_sums, unit_sums, sizes)
    if last:
        summed = later_sum
        scatters.append(Scatter([grad_qkv], sizes))
    return cp_total(partial, brought, last), sums, summed, grad_qkv, scatters


def branch_terms(low, activated, mlp_in, grad_upper, attended, sizes):
    up = dot_tn(mlp_in, grad_upper).astype(BF16)
    down = dot_tn(activated, low).astype(BF16)
    dense = jnp.zeros((sizes.members * sizes.width, sizes.features), BF16)
    dense = lax.dynamic_update_slice_in_dim(
        dense, dot_tn(attended, low).astype(BF16), lax.axis_index("cp") * sizes.width, 0
    )
    return [up, down, dense[: sizes.features]]


def vector_sums(attn_sums, mlp_sums, qkv_bias, up_bias, sizes):
    me = lax.axis_index("cp")
    local, padded = sizes.width, sizes.members * sizes.width
    out_bias = jnp.where(me == 0, mlp_sums[2:3], 0.0)
    rows = [attn_sums[0:1], attn_sums[1:2], mlp_sums[0:1], mlp_sums[1:2], out_bias]
    for part in range(3):
        row = jnp.zeros((1, padded), F32)
        row = lax.dynamic_update_slice(
            row, qkv_bias[0:1, part * local : (part + 1) * local], (0, me * local)
        )
        rows.append(row[:, : HEADS * HEAD_DIM])
    up = jnp.zeros((1, sizes.members * sizes.hidden), F32)
    rows.append(lax.dynamic_update_slice(up, up_bias[0:1], (0, me * sizes.hidden)))
    return jnp.concatenate(rows, axis=1)


def finish_gradients(summed, sizes):
    members, features, hidden, width = sizes.members, sizes.features, sizes.hidden, sizes.width
    rows = summed.shape[0] // members
    down = sizes.unpack_down(summed[:, hidden : 2 * hidden]).astype(BF16)
    down = to_users(down, sizes, back=True).astype(F32)
    joined = jnp.concatenate([summed[:, :hidden], summed[:, 2 * hidden :]], axis=1)
    joined = cp_exchange(joined.reshape(members, rows, -1))
    up = jnp.transpose(joined[:, :, :hidden], (1, 0, 2)).reshape(rows, -1)
    dense = jnp.sum(joined[:, :, hidden : hidden + features], axis=0)
    qkv = joined[:, :, hidden + features :].reshape(members, rows, 3, width)
    qkv = jnp.transpose(qkv, (1, 2, 0, 3)).reshape(rows, 3, members * width)
    qkv = qkv[:, :, : HEADS * HEAD_DIM].reshape(rows, -1)
    return qkv, dense, up, down


def per_device(inputs, doc_ids, cotangent, *params):
    sizes = Sizes(inputs.shape[1], params[8].shape[2])
    small = (0, 1, 2, 3, 5, 7, 9, 11)
    docs = cp_gather(doc_ids)
    exchanged, docs, inputs, cotangent, vectors = lax.optimization_barrier(
        (
            cp_exchange(cut_columns(params, sizes)), docs, inputs, cotangent,
            [params[index] for index in small],
        )
    )
    params = list(params)
    for index, vector in zip(small, vectors):
        params[index] = vector
    tokens = jnp.stack([inputs, cotangent])
    if sizes.members == 2:
        fetched, other = fetch_layers(
            params, exchanged, to_users(params[10], sizes), sizes, cp_peer(tokens)
        )
        first = lax.axis_index("cp") == 0
        both = jnp.stack([jnp.where(first, tokens, other), jnp.where(first, other, tokens)])
    else:
        fetched, tokens = fetch_layers(
            params, exchanged, to_users(params[10], sizes), sizes, tokens
        )
        both = cp_gather(tokens[None])
    vectors = fetch_vectors(params, sizes)
    for layer in range(LAYERS):
        fetched[layer].update(vectors[layer])
    both = both.astype(F32)
    hidden = both[:, 0].reshape(-1, inputs.shape[1])
    low = both[:, 1].reshape(-1, inputs.shape[1]).astype(BF16)
    place = jnp.arange(docs.shape[0], dtype=jnp.int32)
    starts = jnp.sum((docs[None, :] < docs[:, None]).astype(jnp.int32), axis=1)
    tables = rotary_tables(place - starts)
    penalties = document_penalties(docs)
    me = lax.axis_index("cp")
    rows = inputs.shape[0]

    def own_rows(array):
        return lax.dynamic_slice_in_dim(array, me * rows, rows, 0)

    records = []
    for layer in range(LAYERS):
        partial, partial_low, kept = layer_forward(
            hidden, fetched[layer], tables, penalties, sizes
        )
        records.append(kept)
        out_bias = fetched[layer]["out_bias"]
        if layer < LAYERS - 1:
            hidden = hidden + cp_sum(partial, partial_low) + out_bias
        else:
            output = own_rows(hidden) + cp_sum_rows(partial, partial_low) + out_bias
    vector_terms, summed, earlier, layer_sum = [], [], None, None
    upstream = low.astype(F32)
    for layer in reversed(range(LAYERS)):
        total, sums, layer_sum, grad_qkv, scatters = layer_backward(
            low, fetched[layer], records[layer], tables, penalties, sizes, earlier, layer_sum
        )
        vector_terms.append(sums)
        if layer == 0:
            summed[-1:] = [layer_sum]
        else:
            summed.append(layer_sum)
        if layer > 0:
            earlier = (earlier or []) + [grad_qkv]
            upstream = upstream + total
            low = upstream.astype(BF16)
        else:
            input_grad = own_rows(upstream) + total
    flat = sum_everywhere(jnp.concatenate(vector_terms[::-1]))
    finish(scatters)
    mixed, last_qkv = scatters[0].result, scatters[1].result
    first = 2 * sizes.hidden + sizes.features
    width = 3 * sizes.width
    sums = [jnp.concatenate([mixed[:, :first], last_qkv], axis=1)] + [
        jnp.concatenate(
            [
                summed[index].astype(F32),
                mixed[:, first + index * width : first + (index + 1) * width],
            ],
            axis=1,
        )
        for index in range(LAYERS - 1)
    ][::-1]
    qkv, dense, up, down = (
        jnp.stack(grads) for grads in zip(*(finish_gradients(part, sizes) for part in sums))
    )
    owner, features = lax.axis_index("seq") * sizes.members + me, sizes.features
    own, first = [], 0
    for blocks in (1, 1, 1, 1, 1, 3, sizes.ratio):
        share = blocks * sizes.owned
        own.append(lax.dynamic_slice_in_dim(flat, first + owner * share, share, 1))
        first += blocks * features
    gain_attn, bias_attn, gain_mlp, bias_mlp, out_bias, qkv_bias, up_bias = own
    return (
        output.astype(BF16), input_grad, gain_attn, bias_attn, gain_mlp, bias_mlp, qkv, qkv_bias,
        dense, out_bias, up, up_bias, down, out_bias,
    )


def solution(mesh):
    rows, shared = P(("seq", "cp")), P(None, ("seq", "cp"))
    return jax.shard_map(
        per_device,
        mesh=mesh,
        in_specs=(rows,) * 3 + (shared,) * 12,
        out_specs=(rows,) * 2 + (shared,) * 12,
        check_vma=False,
    )
```
